256 devices in a mesh: layer: 16 (over z, core), vocab: 16 (over x, y).
Axes of the slice: x: 4, y: 4, z: 8, core: 2. Of those that a mesh axis runs over, the one named last changes fastest.
Arguments:
- hidden: bfloat16 [16, 32, 2880], P('layer'), may hold values from -6 to 6
- translator: bfloat16 [16, 2880, 2880], P('layer', None, 'vocab'), may hold values from -0.109375 to 0.109375
- bias: float32 [16, 2880], P('layer', 'vocab'), may hold values from -3 to 3
- gain: float32 [2880], P('vocab'), may hold values from 0.1 to 1.9
- unembed: bfloat16 [2880, 200704], P(None, ('layer', 'vocab')), may hold values from -0.3125 to 0.3125
- final_logits: bfloat16 [32, 200704], P(None, ('layer', 'vocab')), may hold values from -230 to 230
Outputs:
- grad_translator: float32 [16, 2880, 2880], P('layer', None, 'vocab')
- grad_bias: float32 [16, 2880], P('layer', 'vocab')
The draws below stay inside these ranges and needn't reach their ends.
All inputs are finite; a program needn't handle non-finite values.
Results may differ from the reference program's by a relative error of at most 0.025.
Values may be sent and summed in bfloat16 or wider, within the bound.
A program may use at most 64 MiB of HBM per device.

```python
import jax
import jax.numpy as jnp
from jax import lax

D = 2880
ROWS = 32
LAYERS = 16
VOCAB = 200704


def draw_final_logits(key, part):
    key = jax.random.fold_in(key, 11)
    key_base = jax.random.fold_in(key, 0)
    values = jnp.clip(3.0 * jax.random.normal(key_base, (ROWS, VOCAB), jnp.float32), -15.0, 15.0)
    return values.astype(jnp.bfloat16)


def block_levels(stream_key, dims, cuts, least, top_value):
    level = 1.0
    for axis_at, blocks in cuts:
        steps = jax.random.uniform(jax.random.fold_in(jax.random.fold_in(stream_key, 6), axis_at), (blocks,), jnp.float32, least / len(cuts), top_value / len(cuts))
        level = level * jnp.repeat(jnp.exp(steps), dims[axis_at] // blocks).reshape((-1,) + (1,) * (len(dims) - 1 - axis_at))
    return level


def normal_values(own_key, shape, spread, most, cuts=(), held_as=jnp.bfloat16):
    result = spread * jax.random.normal(own_key, shape, jnp.float32)
    if cuts:
        result = result * block_levels(own_key, shape, cuts, -0.22, 0.18)
    return jnp.clip(result, -most, most).astype(held_as)


def setup_inputs(seed: int = 0) -> dict:
    key_of = jax.random.split(jax.random.key(seed), 7)
    return {
        "hidden": normal_values(key_of[0], (LAYERS, ROWS, D), 1.0, 6.0, ((0, 16),)),
        "translator": normal_values(key_of[1], (LAYERS, D, D), D ** -0.5, 0.109375, ((0, 16), (2, 16))),
        "bias": normal_values(key_of[2], (LAYERS, D), 0.5, 3.0, ((0, 16), (1, 16)), jnp.float32),
        "gain": jnp.clip(1.0 + 0.18 * jax.random.normal(key_of[3], (D,), jnp.float32), 0.1, 1.9),
        "unembed": normal_values(key_of[4], (D, VOCAB), (D // 9) ** -0.5, 0.3125, ((1, 256),)),
        "final_logits": draw_final_logits(jax.random.fold_in(key_of[6], 71), 0),
    }


eps = 1e-05

def reference(hidden, translator, bias, gain, unembed, final_logits):
    states = hidden.astype(jnp.float32)
    mapped = jnp.stack([jnp.dot(hidden[i], translator[i], preferred_element_type=jnp.float32) for i in range(LAYERS)])
    lens_out = states + mapped + bias[:, None, :]
    inv_rms = lax.rsqrt(lax.optimization_barrier(jnp.mean(lens_out * lens_out, axis=-1, keepdims=True)) + eps)
    normed = (lens_out * inv_rms * gain).astype(jnp.bfloat16)
    logits = jnp.stack([jnp.dot(normed[i], unembed, preferred_element_type=jnp.float32) for i in range(LAYERS)])
    final_f32 = final_logits.astype(jnp.float32)
    row_top = lax.optimization_barrier(jnp.max(final_f32, axis=-1, keepdims=True))
    final_lse = row_top + jnp.log(lax.optimization_barrier(jnp.sum(jnp.exp(final_f32 - row_top), axis=-1, keepdims=True)))
    final_prob = jnp.exp(final_f32 - final_lse)
    lens_lse = jnp.log(lax.optimization_barrier(jnp.sum(jnp.exp(logits), axis=-1, keepdims=True)))
    lens_prob = jnp.exp(logits - lens_lse)
    next_prob = jnp.concatenate([lens_prob[1:], jnp.zeros_like(lens_prob[:1])], axis=0)
    weights = (jnp.arange(LAYERS) < LAYERS - 1).astype(jnp.float32)[:, None, None]
    grad_logits = (lens_prob - final_prob[None] + weights * (lens_prob - next_prob)).astype(jnp.bfloat16)
    unembed_t = unembed.T
    grad_normed = jnp.stack([jnp.dot(grad_logits[i], unembed_t, preferred_element_type=jnp.float32) for i in range(LAYERS)])
    proj = lax.optimization_barrier(jnp.sum(gain * grad_normed * lens_out, axis=-1, keepdims=True))
    grad_out = inv_rms * gain * grad_normed - lens_out * (inv_rms * inv_rms * inv_rms) * proj / D
    grad_low = grad_out.astype(jnp.bfloat16)
    grad_translator = jnp.stack([jnp.dot(hidden[i].T, grad_low[i], preferred_element_type=jnp.float32) for i in range(LAYERS)])
    grad_bias = lax.optimization_barrier(jnp.sum(grad_out, axis=1))
    return (grad_translator, grad_bias)
```

```python
import functools

import jax
import jax.numpy as jnp
from jax import lax
from jax.experimental import pallas as pl
from jax.experimental.pallas import tpu as pltpu
from jax.sharding import PartitionSpec as P

MESH = pl.DeviceIdType.MESH
F32, BF16 = jnp.float32, jnp.bfloat16
EPS = 1e-05
D, ROWS, OWN, SHARD = 2880, 32, 180, 784
WIN, HALF, QUART = 192, 96, 48
STEP = 176
QUAD = 4 * OWN
TILE = 112


def split3(value):
    high = value.astype(BF16).astype(F32)
    rest = value - high
    mid = rest.astype(BF16).astype(F32)
    return high, mid, (rest - mid).astype(BF16).astype(F32)


def kernel(hid_h, trans_h, bias_h, gain_h, un_h, fin_h, out_ref,
           hid, hpad, trans, bias, gain, un, unt, fin, fint,
           lens, zbuf, nt, dense, stat, logits, inv, grad, gt, core_in,
           zx, zz, ra, rb, rc, rd, q, qown, re, rf, rg, rh, fz32, fz16, fzr,
           local, gz_s, gz_r, gx_s, gx_r, gc_s, gc_r, zx_s, zx_r, zz_s, zz_r,
           ce_s, ce_r, rs_s, rs_r, fz_s, fz_r):
    layer, voc = lax.axis_index("layer"), lax.axis_index("vocab")
    z, c = layer // 2, layer % 2
    x, y = voc // 4, voc % 4
    other = 1 - c
    sibling = (z * 2 + other, voc)

    def remote(src, dst, send, recv, device):
        return pltpu.make_async_remote_copy(
            src_ref=src, dst_ref=dst, send_sem=send, recv_sem=recv,
            device_id=device, device_id_type=MESH)

    barrier = pltpu.get_barrier_semaphore()

    def greet(k, _):
        pl.semaphore_signal(barrier, inc=1, device_id=(layer, (voc + k) % 16), device_id_type=MESH)
        pl.semaphore_signal(barrier, inc=1, device_id=((layer + k) % 16, voc), device_id_type=MESH)
        return 0

    lax.fori_loop(1, 16, greet, 0)

    loads = [pltpu.make_async_copy(a, b, local.at[i]) for i, (a, b) in enumerate(
        [(hid_h, hid), (trans_h, trans), (bias_h, bias), (gain_h, gain), (fin_h, fin), (un_h, un)])]
    for load in loads:
        load.start()
    for load in loads[:5]:
        load.wait()

    hpad[...] = jnp.zeros_like(hpad)
    hpad[:, 0:D] = hid[...].astype(F32)
    first = voc * OWN
    tile = first // 128
    near = hpad[:, pl.ds(pl.multiple_of(tile * 128, 128), 384)]
    own = pltpu.roll(near, (384 - (first - tile * 128)) % 384, axis=1)[:, 0:OWN]
    lens_out = own + lax.dot_general(hid[...], trans[...], (((1,), (1,)), ((), ())),
                                     preferred_element_type=F32) + bias[...]
    shift = y * 4
    base = jnp.where(y < 2, 184, 0)
    lens[...] = jnp.zeros_like(lens)
    lens[:, 0:OWN] = lens_out * gain[...]
    pay = pltpu.roll(lens[...], shift, axis=1)
    lens[:, 0:OWN] = lens_out
    squares = jnp.sum(lens_out * lens_out, axis=1, keepdims=True)
    final = fin[...].astype(F32)
    top = jnp.max(final, axis=1, keepdims=True)
    total = jnp.sum(jnp.exp(final - top), axis=1, keepdims=True)
    lane = lax.broadcasted_iota(jnp.int32, (ROWS, 256), 1)
    for k, value in enumerate((*split3(squares), top, *split3(total))):
        pay = jnp.where(lane == base + k, value, pay)
    zbuf[z] = pay.astype(BF16)

    pl.semaphore_wait(barrier, 30)

    def z_copy(k):
        return remote(zbuf.at[z], zbuf.at[z], gz_s.at[k], gz_r.at[k], (((z + k) % 8) * 2 + c, voc))

    for k in range(1, 8):
        z_copy(k).start()

    fint[...] = jnp.concatenate([final] * 4, axis=0).T
    loads[5].wait()
    eye = (lax.broadcasted_iota(jnp.int32, (256, 256), 0)
           == lax.broadcasted_iota(jnp.int32, (256, 256), 1)).astype(BF16)

    def turn(i, _):
        at = pl.multiple_of(i * 256, 256)
        unt[pl.ds(at, 256), :] = lax.dot_general(
            eye, un[:, pl.ds(at, 256)], (((1,), (1,)), ((), ())),
            preferred_element_type=F32).astype(BF16)
        return 0

    lax.fori_loop(0, 11, turn, 0)
    unt[2816:D, :] = lax.dot_general(
        eye[0:64, 0:64], un[:, 2816:D], (((1,), (1,)), ((), ())),
        preferred_element_type=F32).astype(BF16)

    for k in range(1, 8):
        z_copy(k).wait_recv()
    turned = zbuf[...].astype(F32).reshape(256, 256).T.astype(BF16)
    nt[c, 0, x, y] = turned[0:HALF]
    nt[c, 1, y, x] = turned[HALF:WIN]

    def place(h, f, s):
        return (layer, f * 4 + s) if h == 0 else (layer, s * 4 + f)

    ring = []
    for h, (f, s) in enumerate(((x, y), (y, x))):
        ring.append((f, (f + 3) % 4, (f + 1) % 4, (f + 2) % 4, s, (s + 3) % 4, (s + 1) % 4, (s + 2) % 4))

    def along_f(h, k):
        f, fm, fp, fo, s, sm, sp, so = ring[h]
        src = (nt.at[c, h, f, s], nt.at[c, h, f, s],
               nt.at[c, h, fm, s, pl.ds(0, QUART)], nt.at[c, h, fp, s, pl.ds(QUART, QUART)])[k]
        land = (nt.at[c, h, fm, s], nt.at[c, h, fp, s],
                nt.at[c, h, fo, s, pl.ds(0, QUART)], nt.at[c, h, fo, s, pl.ds(QUART, QUART)])[k]
        to = (fp, fm, fp, fm)[k]
        return src, land, gx_s.at[h, k], gx_r.at[h, k], place(h, to, s)

    def along_s(h, j, k):
        f, fm, fp, fo, s, sm, sp, so = ring[h]
        g = (f, fm, fp, fo)[j]
        n = 4 + 4 * j + k
        src = (nt.at[c, h, g, s], nt.at[c, h, g, s],
               nt.at[c, h, g, sm, pl.ds(0, QUART)], nt.at[c, h, g, sp, pl.ds(QUART, QUART)])[k]
        land = (nt.at[c, h, g, sm], nt.at[c, h, g, sp],
                nt.at[c, h, g, so, pl.ds(0, QUART)], nt.at[c, h, g, so, pl.ds(QUART, QUART)])[k]
        to = (sp, sm, sp, sm)[k]
        return src, land, gx_s.at[h, n], gx_r.at[h, n], place(h, f, to)

    def share(h, j):
        f, fm, fp, fo = ring[h][:4]
        g = (f, fm, fp, fo)[j]
        src, land = nt.at[c, h, g], nt.at[other, h, g]
        n = 4 * h + j
        return src, land, gc_s.at[n], gc_r.at[n], sibling

    def go(copy):
        remote(copy[0], copy[0], *copy[2:]).start()

    def come(copy):
        remote(copy[1], copy[1], *copy[2:]).wait_recv()

    def gone(copy):
        remote(copy[0], copy[0], *copy[2:]).wait_send()

    both = (0, 1)
    for h in both:
        for k in (0, 1):
            go(along_f(h, k))
    for h in both:
        for k in (0, 1):
            go(along_s(h, 0, k))
    for h in both:
        for k in (0, 1):
            come(along_f(h, k))
            go(along_f(h, 2 + k))
    for h in both:
        for j in (1, 2):
            for k in (0, 1):
                go(along_s(h, j, k))
    for h in both:
        for k in (0, 1):
            come(along_s(h, 0, k))
            go(along_s(h, 0, 2 + k))
    for h in both:
        for k in (2, 3):
            come(along_f(h, k))
        for k in (0, 1):
            go(along_s(h, 3, k))
    for j in (1, 2):
        for h in both:
            for k in (0, 1):
                come(along_s(h, j, k))
                go(along_s(h, j, 2 + k))
    for h in both:
        for k in (2, 3):
            come(along_s(h, 0, k))
        go(share(h, 0))
    for h in both:
        for k in (0, 1):
            come(along_s(h, 3, k))
            go(along_s(h, 3, 2 + k))
    for j in (1, 2, 3):
        for h in both:
            for k in (2, 3):
                come(along_s(h, j, k))
            go(share(h, j))
    for h in both:
        for j in range(4):
            come(share(h, j))

    row16 = lax.broadcasted_iota(jnp.int32, (16, 256), 0)

    def join(i, _):
        for p in (0, 1):
            for w in range(4):
                at = pl.multiple_of(i * QUAD, 16) + STEP * w
                head = nt[p, 0, i, w, 0:16]
                if w:
                    tail = nt[p, 1, w - 1, i, 80:96]
                    head = jnp.where(row16 < 4 * w, tail.astype(F32), head.astype(F32)).astype(BF16)
                dense[p, pl.ds(at, 16)] = head
                dense[p, pl.ds(at + 16, 80)] = nt[p, 0, i, w, 16:96]
                if w < 3:
                    dense[p, pl.ds(at + 96, 80)] = nt[p, 1, w, i, 0:80]
                else:
                    dense[p, pl.ds(at + 96, 96)] = nt[p, 1, w, i]
                piece = nt[p, 1, w, i, 80:96].astype(F32)[8:16] if w < 2 else nt[p, 0, i, w, 0:16].astype(F32)[0:8]
                stat[p, i * 4 + w] = piece
        return 0

    lax.fori_loop(0, 4, join, 0)

    tops = []
    for p in (0, 1):
        sums = jnp.sum(stat[p], axis=0)
        inv[p] = jnp.broadcast_to(
            lax.rsqrt((sums[0:1] + sums[1:2] + sums[2:3]) / D + EPS), (8, 256))
        tops.append(jnp.max(stat[p], axis=0)[3:4])
    most = jnp.maximum(tops[0], tops[1])
    most = jnp.broadcast_to(jnp.maximum(most[:, 0:128], most[:, 128:256]), (8, 128))
    for turn_by in (32, 64):
        most = jnp.maximum(most, pltpu.roll(most, turn_by, axis=1))
    wide = jnp.concatenate([most, most], axis=1)[0:1]
    sums = jnp.zeros((1, 256), F32)
    for p in (0, 1):
        scaled = jnp.exp(stat[p, :, 3:4, :] - wide[None])
        part = (stat[p, :, 4:5, :] + stat[p, :, 5:6, :] + stat[p, :, 6:7, :]) * scaled
        sums += jnp.sum(part, axis=0)
    sums = jnp.broadcast_to(sums[:, 0:128] + sums[:, 128:256], (8, 128))
    for turn_by in (32, 64):
        sums += pltpu.roll(sums, turn_by, axis=1)
    final_lse = (most + jnp.log(sums))[0:1]

    for n, (at, depth) in enumerate(((0, 768), (768, 768), (1536, 768), (2304, 576))):
        for p in (0, 1):
            part = jnp.dot(un[:, at:at + depth], dense[p, at:at + depth], preferred_element_type=F32)
            if n:
                logits[p] += part
            else:
                logits[p] = part

    def fold(value):
        return jnp.sum(value.reshape(TILE // 8, 8, 256), axis=0)

    def totals(i, carry):
        at = pl.multiple_of(i * TILE, TILE)
        out = []
        for p in (0, 1):
            value = logits[p, pl.ds(at, TILE)] * inv[p, 0:1]
            logits[p, pl.ds(at, TILE)] = value
            out.append(carry[p] + fold(jnp.exp(value)))
        return tuple(out)

    zero = jnp.zeros((8, 256), F32)
    sums = lax.fori_loop(0, SHARD // TILE, totals, (zero, zero))
    sums = [jnp.sum(value, axis=0, keepdims=True) for value in sums]

    zx[voc] = jnp.concatenate(
        [sums[0][:, 0:128], sums[0][:, 128:256], sums[1][:, 0:128], sums[1][:, 128:256],
         jnp.zeros((4, 128), F32)], axis=0)

    def zx_copy(k):
        return remote(zx.at[voc], zx.at[voc], zx_s.at[k], zx_r.at[k], (layer, (voc + k) % 16))

    def zz_copy(k):
        return remote(zz.at[layer], zz.at[layer], zz_s.at[k], zz_r.at[k], ((layer + k) % 16, voc))

    def each(lo, hi, act):
        def body(k, _):
            act(k)
            return 0
        lax.fori_loop(lo, hi, body, 0)

    each(1, 16, lambda k: zx_copy(k).start())
    each(1, 16, lambda k: zx_copy(k).wait_recv())
    zz[layer] = jnp.sum(zx[...], axis=0)
    each(1, 16, lambda k: zz_copy(k).start())
    each(1, 16, lambda k: zz_copy(k).wait_recv())
    lse = jnp.log(jnp.sum(zz[...], axis=0)[0:4])
    lse = [jnp.concatenate([lse[2 * p:2 * p + 1], lse[2 * p + 1:2 * p + 2]], axis=1) for p in (0, 1)]

    last = lax.broadcasted_iota(jnp.int32, (1, 256), 1) < 224

    def slopes(i, carry):
        at = pl.multiple_of(i * TILE, TILE)
        rows = pl.ds(at, TILE)
        x0, x1 = logits[0, rows], logits[1, rows]
        p0, p1 = jnp.exp(x0 - lse[0]), jnp.exp(x1 - lse[1])
        pf = jnp.exp(fint[rows] - final_lse)
        pf = jnp.concatenate([pf, pf], axis=1)
        after = pltpu.roll(p0, 224, axis=1)
        g0 = (p0 - pf) + (p0 - p1)
        g1 = (p1 - pf) + jnp.where(last, p1 - after, 0.0)
        grad[0, rows] = g0.astype(BF16)
        grad[1, rows] = g1.astype(BF16)
        return carry[0] + fold(g0 * x0), carry[1] + fold(g1 * x1)

    proj = lax.fori_loop(0, SHARD // TILE, slopes, (zero, zero))
    tagged = []
    row8 = lax.broadcasted_iota(jnp.int32, (8, 256), 0)
    for p in (0, 1):
        value = jnp.sum(proj[p], axis=0, keepdims=True)
        high = value.astype(BF16).astype(F32)
        tagged.append(jnp.where(row8 == 0, high, value - high))

    def product(p, tag, i):
        rows = pl.ds(pl.multiple_of(i * QUAD, 16), QUAD)
        value = jnp.dot(unt[rows, :], grad[p], preferred_element_type=F32)
        for w in range(4):
            one, two = value[STEP * w:STEP * w + HALF], value[STEP * w + HALF:STEP * w + WIN]
            if w < 2:
                two = jnp.concatenate([two[0:88], jnp.where(row8 < 2, tag, two[88:96])], axis=0)
            else:
                one = jnp.concatenate([jnp.where(row8 < 2, tag, one[0:8]), one[8:96]], axis=0)
            gt[p, 0, i, w] = one.astype(BF16)
            gt[p, 1, w, i] = two.astype(BF16)

    def cross(i, h):
        src = gt.at[other, 0, i] if h == 0 else gt.at[other, 1, :, i]
        land = core_in.at[0, i] if h == 0 else core_in.at[1, :, i]
        n = 4 * h + i
        return remote(src, land, ce_s.at[n], ce_r.at[n], sibling)

    tag_other = jnp.where(c == 0, tagged[1], tagged[0])
    tag_own = jnp.where(c == 0, tagged[0], tagged[1])

    def away(i, _):
        product(other, tag_other, i)
        cross(i, 0).start()
        cross(i, 1).start()
        return 0

    lax.fori_loop(0, 4, away, 0)

    def home(i, _):
        product(c, tag_own, i)
        return 0

    lax.fori_loop(0, 4, home, 0)

    def merge(i, _):
        for h in (0, 1):
            cross(i, h).wait_recv()
        for w in range(4):
            gt[c, 0, i, w] = (gt[c, 0, i, w].astype(F32) + core_in[0, i, w].astype(F32)).astype(BF16)
            gt[c, 1, w, i] = (gt[c, 1, w, i].astype(F32) + core_in[1, w, i].astype(F32)).astype(BF16)
        return 0

    lax.fori_loop(0, 4, merge, 0)

    def add(ref, at, got):
        ref[at] = (ref[at].astype(F32) + got.astype(F32)).astype(BF16)

    def scatter(h, k):
        f, fm, fp, fo, s, sm, sp, so = ring[h]
        lo, hi = pl.ds(0, QUART), pl.ds(QUART, QUART)
        src = (gt.at[c, h, :, so, lo], gt.at[c, h, :, so, hi], gt.at[c, h, :, sp], gt.at[c, h, :, sm],
               q.at[h, fo, lo], q.at[h, fo, hi], q.at[h, fp], q.at[h, fm])[k]
        land = (ra.at[h], rb.at[h], rc.at[h], rd.at[h], re.at[h], rf.at[h], rg.at[h], rh.at[h])[k]
        to = place(h, f, (sp, sm)[k % 2]) if k < 4 else place(h, (fp, fm)[k % 2], s)
        return remote(src, land, rs_s.at[h, k], rs_r.at[h, k], to)

    for h in both:
        scatter(h, 0).start()
        scatter(h, 1).start()
    for h in both:
        f, fm, fp, fo, s, sm, sp, so = ring[h]
        scatter(h, 0).wait_recv()
        for g in range(4):
            add(gt, (c, h, g, sp, pl.ds(0, QUART)), ra[h, g])
        scatter(h, 2).start()
        scatter(h, 1).wait_recv()
        for g in range(4):
            add(gt, (c, h, g, sm, pl.ds(QUART, QUART)), rb[h, g])
        scatter(h, 3).start()
    for h in both:
        f, fm, fp, fo, s, sm, sp, so = ring[h]
        scatter(h, 2).wait_recv()
        scatter(h, 3).wait_recv()
        for g in range(4):
            q[h, g] = (gt[c, h, g, s].astype(F32) + rc[h, g].astype(F32) + rd[h, g].astype(F32)).astype(BF16)
        qown[h] = gt[c, h, f, s].astype(F32) + rc[h, f].astype(F32) + rd[h, f].astype(F32)
        scatter(h, 4).start()
        scatter(h, 5).start()
    for h in both:
        f, fm, fp, fo, s, sm, sp, so = ring[h]
        scatter(h, 4).wait_recv()
        add(q, (h, fp, pl.ds(0, QUART)), re[h])
        scatter(h, 6).start()
        scatter(h, 5).wait_recv()
        add(q, (h, fm, pl.ds(QUART, QUART)), rf[h])
        scatter(h, 7).start()
    whole = []
    for h in both:
        scatter(h, 6).wait_recv()
        scatter(h, 7).wait_recv()
        whole.append(qown[h] + rg[h].astype(F32) + rh[h].astype(F32))

    own_inv = jnp.where(c == 0, inv[0], inv[1])
    full = jnp.concatenate([*whole, own_inv, jnp.zeros((56, 256), F32)], axis=0).T
    fz32[...] = full.reshape(8, ROWS, 256)
    fz16[...] = fz32[...].astype(BF16)

    def fz_copy(k):
        to = (z + k) % 8
        return remote(fz16.at[to], fzr.at[k], fz_s.at[k], fz_r.at[k], (to * 2 + c, voc))

    for k in range(1, 8):
        fz_copy(k).start()
    grown = fz32[z]
    inv_col = grown[:, WIN:WIN + 1]
    for k in range(1, 8):
        fz_copy(k).wait_recv()
        grown += fzr[k].astype(F32)
    along = jnp.sum(jnp.where((lane == base) | (lane == base + 1), grown, 0.0), axis=1, keepdims=True)
    grown = pltpu.roll(grown, (256 - shift) % 256, axis=1)[:, 0:OWN]
    out_ref[...] = inv_col * gain[...] * grown - lens[:, 0:OWN] * (inv_col * inv_col * along / D)

    for k in range(1, 8):
        z_copy(k).wait_send()
        fz_copy(k).wait_send()
    for h in both:
        for k in range(4):
            gone(along_f(h, k))
            for j in range(4):
                gone(along_s(h, j, k))
            gone(share(h, k))
            cross(k, h).wait_send()
        for k in range(8):
            scatter(h, k).wait_send()
    each(1, 16, lambda k: zx_copy(k).wait_send())
    each(1, 16, lambda k: zz_copy(k).wait_send())


def weights(hid_ref, go_ref, out_ref, bias_ref):
    turned = go_ref[...].T
    bias_ref[...] = jnp.sum(go_ref[...], axis=0, keepdims=True)
    value = jnp.dot(turned.astype(BF16), hid_ref[...], preferred_element_type=F32)
    out_ref[...] = value.reshape(out_ref.shape)


def on_device(hidden, translator, bias, gain, unembed, final_logits):
    vmem, sem = pltpu.VMEM, pltpu.SemaphoreType.DMA
    anywhere = pl.BlockSpec(memory_space=pl.ANY)
    inside = pl.BlockSpec(memory_space=pltpu.VMEM)
    grad_out = pl.pallas_call(
        kernel,
        out_shape=jax.ShapeDtypeStruct((ROWS, OWN), F32),
        in_specs=[anywhere] * 6,
        out_specs=inside,
        scratch_shapes=[
            vmem((ROWS, D), BF16), vmem((ROWS, 3072), F32), vmem((OWN, D), BF16),
            vmem((1, OWN), F32), vmem((1, OWN), F32),
            vmem((SHARD, D), BF16), vmem((D, SHARD), BF16),
            vmem((ROWS, SHARD), BF16), vmem((SHARD, 128), F32),
            vmem((ROWS, 256), F32), vmem((8, ROWS, 256), BF16),
            vmem((2, 2, 4, 4, HALF, 256), BF16), vmem((2, D, 256), BF16),
            vmem((2, 16, 8, 256), F32), vmem((2, SHARD, 256), F32), vmem((2, 8, 256), F32),
            vmem((2, SHARD, 256), BF16), vmem((2, 2, 4, 4, HALF, 256), BF16),
            vmem((2, 4, 4, HALF, 256), BF16),
            vmem((16, 8, 128), F32), vmem((16, 8, 128), F32),
            vmem((2, 4, QUART, 256), BF16), vmem((2, 4, QUART, 256), BF16),
            vmem((2, 4, HALF, 256), BF16), vmem((2, 4, HALF, 256), BF16),
            vmem((2, 4, HALF, 256), BF16), vmem((2, HALF, 256), F32),
            vmem((2, QUART, 256), BF16), vmem((2, QUART, 256), BF16),
            vmem((2, HALF, 256), BF16), vmem((2, HALF, 256), BF16),
            vmem((8, ROWS, 256), F32), vmem((8, ROWS, 256), BF16), vmem((8, ROWS, 256), BF16),
            sem((6,)), sem((8,)), sem((8,)), sem((2, 20)), sem((2, 20)), sem((8,)), sem((8,)),
            sem((16,)), sem((16,)), sem((16,)), sem((16,)),
            sem((8,)), sem((8,)), sem((2, 8)), sem((2, 8)), sem((8,)), sem((8,)),
        ],
        compiler_params=pltpu.CompilerParams(
            collective_id=0, has_side_effects=True, vmem_limit_bytes=58 * 1024 * 1024),
    )(hidden[0], translator[0].T, bias, gain.reshape(1, OWN), unembed.T, final_logits)
    grad_translator, grad_bias = pl.pallas_call(
        weights,
        out_shape=(jax.ShapeDtypeStruct((OWN, 1, D), F32), jax.ShapeDtypeStruct((1, OWN), F32)),
        in_specs=[inside, inside],
        out_specs=(inside, inside),
        compiler_params=pltpu.CompilerParams(vmem_limit_bytes=32 * 1024 * 1024),
    )(hidden[0], grad_out)
    return jnp.transpose(grad_translator, (1, 2, 0)), grad_bias


def solution(mesh):
    placed = (
        P("layer", None, None),
        P("layer", None, "vocab"),
        P("layer", "vocab"),
        P("vocab"),
        P(None, ("layer", "vocab")),
        P(None, ("layer", "vocab")),
    )
    return jax.shard_map(
        on_device,
        mesh=mesh,
        in_specs=placed,
        out_specs=(P("layer", None, "vocab"), P("layer", "vocab")),
        check_vma=False,
    )
```

```python
import functools

import jax
import jax.numpy as jnp
from jax import lax
from jax.experimental import pallas as pl
from jax.experimental.pallas import tpu as pltpu
from jax.sharding import PartitionSpec as P

MESH = pl.DeviceIdType.MESH
F32, BF16 = jnp.float32, jnp.bfloat16
EPS = 1e-05
D, ROWS, OWN, SHARD = 2880, 32, 180, 784
WIN, HALF = 192, 96
STEP = 176
QUAD = 4 * OWN
TILE = 112
NEAR = (1, 3, 2)
FAR = (2, 1, 3)


def split3(value):
    high = value.astype(BF16).astype(F32)
    rest = value - high
    mid = rest.astype(BF16).astype(F32)
    return high, mid, (rest - mid).astype(BF16).astype(F32)


def kernel(hid_h, trans_h, bias_h, gain_h, un_h, fin_h, out_ref,
           hid, hpad, trans, bias, gain, un, unt, fin, fint,
           lens, zbuf, nt, dense, stat, logits, inv, grad, gt, core_in,
           zx, zz, sin, q, qown, fzin, fz32, fz16, fzr,
           local, gz_s, gz_r, gf_s, gf_r, gs_s, gs_r, gc_s, gc_r, zx_s, zx_r, zz_s, zz_r,
           ce_s, ce_r, ss_s, ss_r, sf_s, sf_r, fz_s, fz_r):
    layer, voc = lax.axis_index("layer"), lax.axis_index("vocab")
    z, c = layer // 2, layer % 2
    x, y = voc // 4, voc % 4
    other = 1 - c
    sibling = (z * 2 + other, voc)

    def remote(src, dst, send, recv, device):
        return pltpu.make_async_remote_copy(
            src_ref=src, dst_ref=dst, send_sem=send, recv_sem=recv,
            device_id=device, device_id_type=MESH)

    def begin(copy, *at):
        copy(*at).start()

    def sent(ref, semaphore):
        remote(ref, ref, semaphore, semaphore, sibling).wait_send()

    def landed(ref, semaphore):
        remote(ref, ref, semaphore, semaphore, sibling).wait_recv()

    def each(lo, hi, act):
        def body(k, _):
            act(k)
            return 0
        lax.fori_loop(lo, hi, body, 0)

    barrier = pltpu.get_barrier_semaphore()

    def greet(k):
        pl.semaphore_signal(barrier, inc=1, device_id=((layer + k) % 16, voc), device_id_type=MESH)
        pl.semaphore_signal(barrier, inc=1, device_id=(layer, (voc + k) % 16), device_id_type=MESH)

    loads = [pltpu.make_async_copy(a, b, local.at[i]) for i, (a, b) in enumerate(
        [(trans_h, trans), (hid_h, hid), (bias_h, bias), (gain_h, gain), (fin_h, fin)])]
    parts = [pltpu.make_async_copy(un_h.at[pl.ds(i * TILE, TILE)], un.at[pl.ds(i * TILE, TILE)], local.at[5])
             for i in range(SHARD // TILE)]
    for load in loads:
        load.start()
    each(1, 16, greet)

    loads[4].wait()
    final = fin[...].astype(F32)
    top = jnp.max(final, axis=1, keepdims=True)
    total = jnp.sum(jnp.exp(final - top), axis=1, keepdims=True)

    for load in loads[:4]:
        load.wait()
    hpad[:, 2688:3072] = jnp.zeros((ROWS, 384), F32)
    hpad[:, 0:D] = hid[...].astype(F32)
    first = voc * OWN
    tile = first // 128
    near = hpad[:, pl.ds(pl.multiple_of(tile * 128, 128), 384)]
    own = pltpu.roll(near, (384 - (first - tile * 128)) % 384, axis=1)[:, 0:OWN]
    lens_out = own + lax.dot_general(hid[...], trans[...], (((1,), (1,)), ((), ())),
                                     preferred_element_type=F32) + bias[...]
    shift = y * 4
    base = jnp.where(y < 2, 184, 0)
    lens[...] = jnp.zeros_like(lens)
    lens[:, 0:OWN] = lens_out * gain[...]
    pay = pltpu.roll(lens[...], shift, axis=1)
    lens[:, 0:OWN] = lens_out
    squares = jnp.sum(lens_out * lens_out, axis=1, keepdims=True)
    lane = lax.broadcasted_iota(jnp.int32, (ROWS, 256), 1)
    for k, value in enumerate((*split3(squares), top, *split3(total))):
        pay = jnp.where(lane == base + k, value, pay)
    zbuf[z] = pay.astype(BF16)

    pl.semaphore_wait(barrier, 30)

    def z_send(k):
        return remote(zbuf.at[z], zbuf.at[z], gz_s.at[0], gz_r.at[z // 4], (((z + k) % 8) * 2 + c, voc))

    def z_come(g):
        @pl.when(z // 4 == g)
        def _():
            landed(zbuf.at[pl.ds(4 * g, 3)], gz_r.at[g])

        @pl.when(z // 4 != g)
        def _():
            landed(zbuf.at[pl.ds(4 * g, 4)], gz_r.at[g])

    for k in (4, 3, 5, 2, 6, 1, 7):
        begin(z_send, k)
    for part in parts:
        part.start()

    axes = ((x, y), (y, x))

    def place(h, f, s):
        return (layer, f * 4 + s) if h == 0 else (layer, s * 4 + f)

    def f_send(g, h, k):
        f, s = axes[h]
        src = nt.at[c, g, h, f, s]
        return remote(src, src, gf_s.at[0], gf_r.at[g, h, k - 1], place(h, (f + k) % 4, s))

    def f_come(g, h, k):
        f, s = axes[h]
        land = nt.at[c, g, h, (f + 4 - k) % 4, s]
        landed(land, gf_r.at[g, h, k - 1])

    def s_send(g, h, j, k):
        f, s = axes[h]
        src = nt.at[c, g, h, (f + 4 - j) % 4, s]
        return remote(src, src, gs_s.at[0], gs_r.at[g, h, j], place(h, f, (s + k) % 4))

    def s_come(g, h, j):
        f, s = axes[h]
        landed(nt.at[c, g, h, (f + 4 - j) % 4, pl.ds(0, 3)], gs_r.at[g, h, j])

    def share(g, h, j):
        f, s = axes[h]
        src = nt.at[c, g, h, (f + 4 - j) % 4]
        return remote(src, src, gc_s.at[0], gc_r.at[g], sibling)

    def share_come(g):
        landed(nt.at[other, g], gc_r.at[g])

    both = (0, 1)

    def gather_own(g):
        z_come(g)
        turned = zbuf[4 * g:4 * g + 4].astype(F32).reshape(128, 256).T.astype(BF16)
        nt[c, g, 0, x, y] = turned[0:HALF]
        nt[c, g, 1, y, x] = turned[HALF:WIN]
        for k in FAR:
            for h in both:
                begin(f_send, g, h, k)
        for k in FAR:
            for h in both:
                begin(s_send, g, h, 0, k)

    def gather_on(g):
        for j in NEAR:
            for h in both:
                f_come(g, h, j)
                for k in FAR:
                    begin(s_send, g, h, j, k)

    def gather_end(g):
        for j in (0, *NEAR):
            for h in both:
                s_come(g, h, j)
                begin(share, g, h, j)

    row16 = lax.broadcasted_iota(jnp.int32, (16, 128), 0)

    def join(g):
        def body(i):
            for p in both:
                cols = slice(128 * p, 128 * p + 128)
                for w in range(4):
                    at = pl.multiple_of(i * QUAD, 16) + STEP * w
                    head = nt[p, g, 0, i, w, 0:16]
                    if w:
                        tail = nt[p, g, 1, w - 1, i, 80:96]
                        head = jnp.where(row16 < 4 * w, tail.astype(F32), head.astype(F32)).astype(BF16)
                    dense[g, pl.ds(at, 16), cols] = head
                    dense[g, pl.ds(at + 16, 80), cols] = nt[p, g, 0, i, w, 16:96]
                    if w < 3:
                        dense[g, pl.ds(at + 96, 80), cols] = nt[p, g, 1, w, i, 0:80]
                    else:
                        dense[g, pl.ds(at + 96, 96), cols] = nt[p, g, 1, w, i]
                    if w < 2:
                        piece = nt[p, g, 1, w, i, 80:96].astype(F32)[8:16]
                    else:
                        piece = nt[p, g, 0, i, w, 0:16].astype(F32)[0:8]
                    stat[g, i * 4 + w, :, cols] = piece

        each(0, 4, body)
        sums = jnp.sum(stat[g], axis=0)
        inv[g] = jnp.broadcast_to(lax.rsqrt((sums[0:1] + sums[1:2] + sums[2:3]) / D + EPS), (8, 256))

    def fold(value):
        return jnp.sum(value.reshape(TILE // 8, 8, 256), axis=0)

    zero = jnp.zeros((8, 256), F32)

    def forward(g):
        for n, (at, depth) in enumerate(((0, 768), (768, 768), (1536, 768), (2304, 576))):
            part = jnp.dot(un[:, at:at + depth], dense[g, at:at + depth], preferred_element_type=F32)
            if n:
                logits[g] += part
            else:
                logits[g] = part

        def body(i, carry):
            rows = pl.ds(pl.multiple_of(i * TILE, TILE), TILE)
            value = logits[g, rows] * inv[g, 0:1]
            logits[g, rows] = value
            return carry + fold(jnp.exp(value))

        sums = jnp.sum(lax.fori_loop(0, SHARD // TILE, body, zero), axis=0, keepdims=True)
        zx[g, 0] = jnp.concatenate([sums[:, 0:128], sums[:, 128:256]], axis=0)

    def zx_copy(g, k):
        return remote(zx.at[g, 0], zx.at[g, k], zx_s.at[0], zx_r.at[g], (layer, (voc + k) % 16))

    def zz_copy(g, k):
        return remote(zz.at[g, 0], zz.at[g, k], zz_s.at[0], zz_r.at[g], ((layer + k) % 16, voc))

    def all_of(copy, g):
        each(1, 16, lambda k: copy(g, k).start())


    eye = (lax.broadcasted_iota(jnp.int32, (256, 256), 0)
           == lax.broadcasted_iota(jnp.int32, (256, 256), 1)).astype(BF16)

    def turn(i):
        at = pl.multiple_of(i * 256, 256)
        unt[pl.ds(at, 256), :] = lax.dot_general(
            eye, un[:, pl.ds(at, 256)], (((1,), (1,)), ((), ())),
            preferred_element_type=F32).astype(BF16)

    def turn_last():
        unt[2816:D, :] = lax.dot_general(
            eye[0:64, 0:64], un[:, 2816:D], (((1,), (1,)), ((), ())),
            preferred_element_type=F32).astype(BF16)

    gather_own(1)
    gather_own(0)
    gather_on(1)
    pltpu.make_async_copy(un_h, un, local.at[5]).wait()
    each(0, 4, turn)
    gather_on(0)
    each(4, 7, turn)
    gather_end(1)
    share_come(1)
    join(1)
    forward(1)
    all_of(zx_copy, 1)
    each(7, 11, turn)
    turn_last()
    gather_end(0)
    share_come(0)
    join(0)
    forward(0)
    all_of(zx_copy, 0)
    landed(zx.at[1, pl.ds(1, 15)], zx_r.at[1])
    zz[1, 0] = jnp.sum(zx[1], axis=0)
    all_of(zz_copy, 1)

    fint[...] = jnp.concatenate([final] * 4, axis=0).T
    most = jnp.maximum(jnp.max(stat[0], axis=0), jnp.max(stat[1], axis=0))[3:4]
    most = jnp.broadcast_to(jnp.maximum(most[:, 0:128], most[:, 128:256]), (8, 128))
    for turn_by in (32, 64):
        most = jnp.maximum(most, pltpu.roll(most, turn_by, axis=1))
    wide = jnp.concatenate([most, most], axis=1)[0:1]
    sums = jnp.zeros((1, 256), F32)
    for g in both:
        scaled = jnp.exp(stat[g, :, 3:4, :] - wide[None])
        part = (stat[g, :, 4:5, :] + stat[g, :, 5:6, :] + stat[g, :, 6:7, :]) * scaled
        sums += jnp.sum(part, axis=0)
    sums = jnp.broadcast_to(sums[:, 0:128] + sums[:, 128:256], (8, 128))
    for turn_by in (32, 64):
        sums += pltpu.roll(sums, turn_by, axis=1)
    final_lse = (most + jnp.log(sums))[0:1]

    landed(zx.at[0, pl.ds(1, 15)], zx_r.at[0])
    zz[0, 0] = jnp.sum(zx[0], axis=0)
    all_of(zz_copy, 0)

    lane128 = lax.broadcasted_iota(jnp.int32, (1, 128), 1)
    row8 = lax.broadcasted_iota(jnp.int32, (8, 256), 0)

    def log_total(g):
        value = jnp.log(jnp.sum(zz[g], axis=0))
        return jnp.concatenate([value[0:1], value[1:2]], axis=1)

    def slopes(g, lse, ahead):
        def body(i, carry):
            rows = pl.ds(pl.multiple_of(i * TILE, TILE), TILE)
            value = logits[g, rows]
            prob = jnp.exp(value - lse)
            target = jnp.exp(fint[rows] - final_lse)
            target = jnp.concatenate([target, target], axis=1)
            p0, p1 = prob[:, 0:128], prob[:, 128:256]
            if ahead is None:
                follow = jnp.where(lane128 < 96, p1 - pltpu.roll(p0, 96, axis=1), 0.0)
            else:
                border = jnp.exp(logits[1, rows, 0:128] - ahead[:, 0:128])
                follow = p1 - pltpu.roll(jnp.where(lane128 < 32, border, p0), 96, axis=1)
            slope = (prob - target) + jnp.concatenate([p0 - p1, follow], axis=1)
            grad[g, rows] = slope.astype(BF16)
            return carry + fold(slope * value)

        proj = jnp.sum(lax.fori_loop(0, SHARD // TILE, body, zero), axis=0, keepdims=True)
        high = proj.astype(BF16).astype(F32)
        return jnp.where(row8 == 0, high, proj - high)

    def product(g, tag, i):
        rows = pl.ds(pl.multiple_of(i * QUAD, 16), QUAD)
        value = jnp.dot(unt[rows, :], grad[g], preferred_element_type=F32)
        for w in range(4):
            one, two = value[STEP * w:STEP * w + HALF], value[STEP * w + HALF:STEP * w + WIN]
            if w < 2:
                two = jnp.concatenate([two[0:88], jnp.where(row8 < 2, tag, two[88:96])], axis=0)
            else:
                one = jnp.concatenate([jnp.where(row8 < 2, tag, one[0:8]), one[8:96]], axis=0)
            one, two = one.astype(BF16), two.astype(BF16)
            for p in both:
                gt[p, g, 0, i, w] = one[:, 128 * p:128 * p + 128]
                gt[p, g, 1, w, i] = two[:, 128 * p:128 * p + 128]

    def cross(g, h, d):
        i = (x + d) % 4
        src = gt.at[other, g, 0, i] if h == 0 else gt.at[other, g, 1, :, i]
        land = core_in.at[g, 0, i] if h == 0 else core_in.at[g, 1, :, i]
        return remote(src, land, ce_s.at[0], ce_r.at[g, d], sibling)

    def s_back(g, h, j, k):
        f, s = axes[h]
        to = (s + k) % 4
        if h == 0:
            n = (f + j) % 4
            return remote(gt.at[c, g, 0, n, to], sin.at[g, 0, k, n], ss_s.at[0], ss_r.at[g, 0],
                          place(h, f, to))
        return remote(gt.at[c, g, 1, :, to], sin.at[g, 1, k], ss_s.at[0], ss_r.at[g, 1],
                      place(h, f, to))

    def merge(g, d):
        i = (x + d) % 4
        landed(core_in.at[g, :, 0], ce_r.at[g, d])
        for w in range(4):
            gt[c, g, 0, i, w] = (gt[c, g, 0, i, w].astype(F32) + core_in[g, 0, i, w].astype(F32)).astype(BF16)
            gt[c, g, 1, w, i] = (gt[c, g, 1, w, i].astype(F32) + core_in[g, 1, w, i].astype(F32)).astype(BF16)
        for k in FAR:
            begin(s_back, g, 0, d, k)
        if d:
            begin(s_back, g, 1, 0, d)

    order = (2, 1, 3, 0)

    def backward(g, tag):
        for n, d in enumerate(order):
            product(g, tag, (x + d) % 4)
            for h in both:
                begin(cross, g, h, d)
            if n:
                merge(g, order[n - 1])
        merge(g, order[3])

    def f_back(g, h, k):
        f, s = axes[h]
        to = (f + k) % 4
        return remote(q.at[g, h, to], fzin.at[g, h, k], sf_s.at[0], sf_r.at[g, h], place(h, to, s))

    def scatter_s(g):
        for h in (1, 0):
            f, s = axes[h]
            landed(sin.at[g, h, pl.ds(1, 3)], ss_r.at[g, h])

            def total_of(n):
                value = gt[c, g, h, n, s].astype(F32)
                for k in (1, 2, 3):
                    value += sin[g, h, k, n].astype(F32)
                return value

            for k in FAR:
                n = (f + k) % 4
                q[g, h, n] = total_of(n).astype(BF16)
                begin(f_back, g, h, k)
            qown[g, h] = total_of(f)

    def fz_copy(g, k):
        to = 4 * g + k
        return remote(fz16.at[to], fzr.at[(to + 8 - z) % 8], fz_s.at[0], fz_r.at[0], (to * 2 + c, voc))

    def scatter_f(g):
        whole = []
        for h in both:
            landed(fzin.at[g, h, pl.ds(1, 3)], sf_r.at[g, h])
            whole.append(qown[g, h] + fzin[g, h, 1].astype(F32) + fzin[g, h, 2].astype(F32)
                         + fzin[g, h, 3].astype(F32))
        own_inv = jnp.where(c == 0, inv[g, :, 0:128], inv[g, :, 128:256])
        full = jnp.concatenate([*whole, own_inv, jnp.zeros((56, 128), F32)], axis=0).T
        fz32[4 * g:4 * g + 4] = full.reshape(4, ROWS, 256)
        fz16[4 * g:4 * g + 4] = full.reshape(4, ROWS, 256).astype(BF16)
        for k in range(4):
            @pl.when(z != 4 * g + k)
            def _():
                fz_copy(g, k).start()

    landed(zz.at[1, pl.ds(1, 15)], zz_r.at[1])
    lse1 = log_total(1)
    tag1 = slopes(1, lse1, None)
    backward(1, tag1)
    landed(zz.at[0, pl.ds(1, 15)], zz_r.at[0])
    tag0 = slopes(0, log_total(0), lse1)
    for n, d in enumerate(order):
        product(0, tag0, (x + d) % 4)
        for h in both:
            begin(cross, 0, h, d)
        if n == 1:
            scatter_s(1)
        if n:
            merge(0, order[n - 1])
    merge(0, order[3])
    scatter_f(1)
    scatter_s(0)
    scatter_f(0)

    grown = fz32[z]
    inv_col = grown[:, WIN:WIN + 1]
    landed(fzr.at[pl.ds(1, 7)], fz_r.at[0])
    for k in range(1, 8):
        grown += fzr[k].astype(F32)
    along = jnp.sum(jnp.where((lane == base) | (lane == base + 1), grown, 0.0), axis=1, keepdims=True)
    grown = pltpu.roll(grown, (256 - shift) % 256, axis=1)[:, 0:OWN]
    out_ref[...] = inv_col * gain[...] * grown - lens[:, 0:OWN] * (inv_col * inv_col * along / D)

    sent(zbuf.at[pl.ds(0, 7)], gz_s.at[0])
    sent(nt.at[c, :, :, 0, pl.ds(0, 3)], gf_s.at[0])
    sent(nt.at[c, :, :, pl.ds(0, 3)], gs_s.at[0])
    sent(nt.at[c], gc_s.at[0])
    sent(zx.at[:, pl.ds(1, 15)], zx_s.at[0])
    sent(zz.at[:, pl.ds(1, 15)], zz_s.at[0])
    sent(gt.at[other], ce_s.at[0])
    sent(gt.at[c, :, :, pl.ds(0, 3)], ss_s.at[0])
    sent(q.at[:, :, pl.ds(0, 3)], sf_s.at[0])
    sent(fz16.at[pl.ds(0, 7)], fz_s.at[0])


def weights(hid_ref, go_ref, out_ref, bias_ref):
    turned = go_ref[...].T
    bias_ref[...] = jnp.sum(go_ref[...], axis=0, keepdims=True)
    value = jnp.dot(turned.astype(BF16), hid_ref[...], preferred_element_type=F32)
    out_ref[...] = value.reshape(out_ref.shape)


def on_device(hidden, translator, bias, gain, unembed, final_logits):
    vmem, sem = pltpu.VMEM, pltpu.SemaphoreType.DMA
    anywhere = pl.BlockSpec(memory_space=pl.ANY)
    inside = pl.BlockSpec(memory_space=pltpu.VMEM)
    grad_out = pl.pallas_call(
        kernel,
        out_shape=jax.ShapeDtypeStruct((ROWS, OWN), F32),
        in_specs=[anywhere] * 6,
        out_specs=inside,
        scratch_shapes=[
            vmem((ROWS, D), BF16), vmem((ROWS, 3072), F32), vmem((OWN, D), BF16),
            vmem((1, OWN), F32), vmem((1, OWN), F32),
            vmem((SHARD, D), BF16), vmem((D, SHARD), BF16),
            vmem((ROWS, SHARD), BF16), vmem((SHARD, 128), F32),
            vmem((ROWS, 256), F32), vmem((8, ROWS, 256), BF16),
            vmem((2, 2, 2, 4, 4, HALF, 128), BF16), vmem((2, D, 256), BF16),
            vmem((2, 16, 8, 256), F32), vmem((2, SHARD, 256), F32), vmem((2, 8, 256), F32),
            vmem((2, SHARD, 256), BF16), vmem((2, 2, 2, 4, 4, HALF, 128), BF16),
            vmem((2, 2, 4, 4, HALF, 128), BF16),
            vmem((2, 16, 2, 128), F32), vmem((2, 16, 2, 128), F32),
            vmem((2, 2, 4, 4, HALF, 128), BF16),
            vmem((2, 2, 4, HALF, 128), BF16), vmem((2, 2, HALF, 128), F32),
            vmem((2, 2, 4, HALF, 128), BF16),
            vmem((8, ROWS, 256), F32), vmem((8, ROWS, 256), BF16), vmem((8, ROWS, 256), BF16),
            sem((6,)), sem((1,)), sem((2,)), sem((1,)), sem((2, 2, 3)),
            sem((1,)), sem((2, 2, 4)), sem((1,)), sem((2,)), sem((1,)), sem((2,)), sem((1,)), sem((2,)),
            sem((1,)), sem((2, 4)), sem((1,)), sem((2, 2)),
            sem((1,)), sem((2, 2)), sem((1,)), sem((1,)),
        ],
        compiler_params=pltpu.CompilerParams(
            collective_id=0, has_side_effects=True, vmem_limit_bytes=58 * 1024 * 1024),
    )(hidden[0], translator[0].T, bias, gain.reshape(1, OWN), unembed.T, final_logits)
    grad_translator, grad_bias = pl.pallas_call(
        weights,
        out_shape=(jax.ShapeDtypeStruct((OWN, 1, D), F32), jax.ShapeDtypeStruct((1, OWN), F32)),
        in_specs=[inside, inside],
        out_specs=(inside, inside),
        compiler_params=pltpu.CompilerParams(vmem_limit_bytes=32 * 1024 * 1024),
    )(hidden[0], grad_out)
    return jnp.transpose(grad_translator, (1, 2, 0)), grad_bias


def solution(mesh):
    placed = (
        P("layer", None, None),
        P("layer", None, "vocab"),
        P("layer", "vocab"),
        P("vocab"),
        P(None, ("layer", "vocab")),
        P(None, ("layer", "vocab")),
    )
    return jax.shard_map(
        on_device,
        mesh=mesh,
        in_specs=placed,
        out_specs=(P("layer", None, "vocab"), P("layer", "vocab")),
        check_vma=False,
    )
```

```python
import functools

import jax
import jax.numpy as jnp
from jax import lax
from jax.experimental import pallas as pl
from jax.experimental.pallas import tpu as pltpu
from jax.sharding import PartitionSpec as P

MESH = pl.DeviceIdType.MESH
F32, BF16 = jnp.float32, jnp.bfloat16
EPS = 1e-05
D, ROWS, OWN, SHARD = 2880, 32, 180, 784
WIN, HALF = 192, 96
STEP = 176
QUAD = 4 * OWN
TILE = 112
NEAR = (1, 3, 2)
FAR = (2, 1, 3)
PLANE = (10, 9, 11, 6, 14, 5, 7, 8, 2, 13, 15, 1, 3, 4, 12)
LINE = (8, 9, 7, 6, 10, 11, 5, 4, 12, 13, 3, 2, 14, 15, 1)


def split3(value):
    high = value.astype(BF16).astype(F32)
    rest = value - high
    mid = rest.astype(BF16).astype(F32)
    return high, mid, (rest - mid).astype(BF16).astype(F32)


def kernel(hid_h, trans_h, bias_h, gain_h, un_h, fin_h, out_ref,
           hid, hpad, trans, bias, gain, un, unt, fin, fint,
           lens, zbuf, nt, dense, stat, logits, inv, grad, gt, core_in,
           border, zx, zz, sin, q, qown, fzin, fz32, fz16, fzr,
           local, gz_s, gz_r, gf_s, gf_r, gs_s, gs_r, gc_s, gc_r, zx_s, zx_r, zz_s, zz_r,
           ce_s, ce_r, ss_s, ss_r, sf_s, sf_r, fz_s, fz_r):
    layer, voc = lax.axis_index("layer"), lax.axis_index("vocab")
    z, c = layer // 2, layer % 2
    x, y = voc // 4, voc % 4
    other = 1 - c
    sibling = (z * 2 + other, voc)

    def remote(src, dst, send, recv, device):
        return pltpu.make_async_remote_copy(
            src_ref=src, dst_ref=dst, send_sem=send, recv_sem=recv,
            device_id=device, device_id_type=MESH)

    def begin(copy, *at):
        copy(*at).start()

    def sent(ref, semaphore):
        remote(ref, ref, semaphore, semaphore, sibling).wait_send()

    def landed(ref, semaphore):
        remote(ref, ref, semaphore, semaphore, sibling).wait_recv()

    def each(lo, hi, act):
        def body(k, _):
            act(k)
            return 0
        lax.fori_loop(lo, hi, body, 0)

    barrier = pltpu.get_barrier_semaphore()

    def greet(k):
        pl.semaphore_signal(barrier, inc=1, device_id=((layer + k) % 16, voc), device_id_type=MESH)
        pl.semaphore_signal(barrier, inc=1, device_id=(layer, (voc + k) % 16), device_id_type=MESH)

    loads = [pltpu.make_async_copy(a, b, local.at[i]) for i, (a, b) in enumerate(
        [(trans_h, trans), (hid_h, hid), (bias_h, bias), (gain_h, gain), (fin_h, fin)])]
    parts = [pltpu.make_async_copy(un_h.at[pl.ds(i * TILE, TILE)], un.at[pl.ds(i * TILE, TILE)], local.at[5])
             for i in range(SHARD // TILE)]
    for load in loads:
        load.start()
    each(1, 16, greet)

    loads[4].wait()
    final = fin[...].astype(F32)
    top = jnp.max(final, axis=1, keepdims=True)
    total = jnp.sum(jnp.exp(final - top), axis=1, keepdims=True)

    for load in loads[:4]:
        load.wait()
    hpad[:, 2688:3072] = jnp.zeros((ROWS, 384), F32)
    hpad[:, 0:D] = hid[...].astype(F32)
    first = voc * OWN
    tile = first // 128
    near = hpad[:, pl.ds(pl.multiple_of(tile * 128, 128), 384)]
    own = pltpu.roll(near, (384 - (first - tile * 128)) % 384, axis=1)[:, 0:OWN]
    lens_out = own + lax.dot_general(hid[...], trans[...], (((1,), (1,)), ((), ())),
                                     preferred_element_type=F32) + bias[...]
    shift = y * 4
    base = jnp.where(y < 2, 184, 0)
    lens[...] = jnp.zeros_like(lens)
    lens[:, 0:OWN] = lens_out * gain[...]
    pay = pltpu.roll(lens[...], shift, axis=1)
    lens[:, 0:OWN] = lens_out
    squares = jnp.sum(lens_out * lens_out, axis=1, keepdims=True)
    lane = lax.broadcasted_iota(jnp.int32, (ROWS, 256), 1)
    for k, value in enumerate((*split3(squares), top, *split3(total))):
        pay = jnp.where(lane == base + k, value, pay)
    zbuf[z] = pay.astype(BF16)

    pl.semaphore_wait(barrier, 30)

    def z_send(k):
        return remote(zbuf.at[z], zbuf.at[z], gz_s.at[0], gz_r.at[z // 4], (((z + k) % 8) * 2 + c, voc))

    def z_come(g):
        @pl.when(z // 4 == g)
        def _():
            landed(zbuf.at[pl.ds(4 * g, 3)], gz_r.at[g])

        @pl.when(z // 4 != g)
        def _():
            landed(zbuf.at[pl.ds(4 * g, 4)], gz_r.at[g])

    for k in (4, 3, 5, 2, 6, 1, 7):
        begin(z_send, k)
    for part in parts:
        part.start()

    axes = ((x, y), (y, x))

    def place(h, f, s):
        return (layer, f * 4 + s) if h == 0 else (layer, s * 4 + f)

    def f_send(g, h, k):
        f, s = axes[h]
        src = nt.at[c, g, h, f, s]
        return remote(src, src, gf_s.at[0], gf_r.at[g, h, k - 1], place(h, (f + k) % 4, s))

    def f_come(g, h, k):
        f, s = axes[h]
        land = nt.at[c, g, h, (f + 4 - k) % 4, s]
        landed(land, gf_r.at[g, h, k - 1])

    def s_send(g, h, j, k):
        f, s = axes[h]
        src = nt.at[c, g, h, (f + 4 - j) % 4, s]
        return remote(src, src, gs_s.at[0], gs_r.at[g, h, j], place(h, f, (s + k) % 4))

    def s_come(g, h, j):
        f, s = axes[h]
        landed(nt.at[c, g, h, (f + 4 - j) % 4, pl.ds(0, 3)], gs_r.at[g, h, j])

    def share(g, h, j):
        f, s = axes[h]
        src = nt.at[c, g, h, (f + 4 - j) % 4]
        return remote(src, src, gc_s.at[0], gc_r.at[g], sibling)

    def share_come(g):
        landed(nt.at[other, g], gc_r.at[g])

    both = (0, 1)

    def gather_own(g):
        z_come(g)
        turned = zbuf[4 * g:4 * g + 4].astype(F32).reshape(128, 256).T.astype(BF16)
        nt[c, g, 0, x, y] = turned[0:HALF]
        nt[c, g, 1, y, x] = turned[HALF:WIN]
        for k in FAR:
            for h in both:
                begin(f_send, g, h, k)
        for k in FAR:
            for h in both:
                begin(s_send, g, h, 0, k)

    def gather_on(g):
        for j in NEAR:
            for h in both:
                f_come(g, h, j)
                for k in FAR:
                    begin(s_send, g, h, j, k)

    def gather_end_part(g, n):
        for h in both:
            s_come(g, h, (0, *NEAR)[n])
            begin(share, g, h, (0, *NEAR)[n])

    def gather_end(g):
        for n in range(4):
            gather_end_part(g, n)

    row16 = lax.broadcasted_iota(jnp.int32, (16, 128), 0)

    def join(g, p):
        cols = pl.ds(pl.multiple_of(128 * p, 128), 128)

        def body(i):
            if True:
                for w in range(4):
                    at = pl.multiple_of(i * QUAD, 16) + STEP * w
                    head = nt[p, g, 0, i, w, 0:16]
                    if w:
                        tail = nt[p, g, 1, w - 1, i, 80:96]
                        head = jnp.where(row16 < 4 * w, tail.astype(F32), head.astype(F32)).astype(BF16)
                    dense[g, pl.ds(at, 16), cols] = head
                    dense[g, pl.ds(at + 16, 80), cols] = nt[p, g, 0, i, w, 16:96]
                    if w < 3:
                        dense[g, pl.ds(at + 96, 80), cols] = nt[p, g, 1, w, i, 0:80]
                    else:
                        dense[g, pl.ds(at + 96, 96), cols] = nt[p, g, 1, w, i]
                    if w < 2:
                        piece = nt[p, g, 1, w, i, 80:96].astype(F32)[8:16]
                    else:
                        piece = nt[p, g, 0, i, w, 0:16].astype(F32)[0:8]
                    stat[g, i * 4 + w, :, cols] = piece

        each(0, 4, body)

    def norms(g):
        sums = jnp.sum(stat[g], axis=0)
        inv[g] = jnp.broadcast_to(lax.rsqrt((sums[0:1] + sums[1:2] + sums[2:3]) / D + EPS), (8, 256))

    def fold(value):
        return jnp.sum(value.reshape(TILE // 8, 8, 256), axis=0)

    zero = jnp.zeros((8, 256), F32)

    def product_of(g, n):
        at, depth = ((0, 768), (768, 768), (1536, 768), (2304, 576))[n]
        part = jnp.dot(un[:, at:at + depth], dense[g, at:at + depth], preferred_element_type=F32)
        if n:
            logits[g] += part
        else:
            logits[g] = part

    def exps(g):
        def body(i, carry):
            rows = pl.ds(pl.multiple_of(i * TILE, TILE), TILE)
            value = logits[g, rows] * inv[g, 0:1]
            logits[g, rows] = value
            return carry + fold(jnp.exp(value))

        sums = jnp.sum(lax.fori_loop(0, SHARD // TILE, body, zero), axis=0, keepdims=True)
        zx[g, 0] = jnp.concatenate([sums[:, 0:128], sums[:, 128:256]], axis=0)

    def zx_copy(g, k):
        return remote(zx.at[g, 0], zx.at[g, k], zx_s.at[0], zx_r.at[g], (layer, (voc + k) % 16))

    def zz_copy(g, k):
        return remote(zz.at[g, 0], zz.at[g, k], zz_s.at[0], zz_r.at[g], ((layer + k) % 16, voc))

    def all_of(copy, g):
        for k in PLANE if copy is zx_copy else LINE:
            copy(g, k).start()


    eye = (lax.broadcasted_iota(jnp.int32, (256, 256), 0)
           == lax.broadcasted_iota(jnp.int32, (256, 256), 1)).astype(BF16)

    def turn(i):
        at = pl.multiple_of(i * 256, 256)
        unt[pl.ds(at, 256), :] = lax.dot_general(
            eye, un[:, pl.ds(at, 256)], (((1,), (1,)), ((), ())),
            preferred_element_type=F32).astype(BF16)

    def turn_last():
        unt[2816:D, :] = lax.dot_general(
            eye[0:64, 0:64], un[:, 2816:D], (((1,), (1,)), ((), ())),
            preferred_element_type=F32).astype(BF16)

    gather_own(1)
    gather_own(0)
    gather_on(1)
    gather_on(0)
    pltpu.make_async_copy(un_h, un, local.at[5]).wait()
    each(0, 4, turn)
    gather_end(1)
    join(1, c)
    share_come(1)
    join(1, other)
    norms(1)
    for n in range(4):
        product_of(1, n)
        gather_end_part(0, n)
    exps(1)
    all_of(zx_copy, 1)
    join(0, c)
    share_come(0)
    join(0, other)
    norms(0)
    for n in range(4):
        product_of(0, n)
    exps(0)
    all_of(zx_copy, 0)
    landed(zx.at[1, pl.ds(1, 15)], zx_r.at[1])
    zz[1, 0] = jnp.sum(zx[1], axis=0)
    all_of(zz_copy, 1)

    fint[...] = jnp.concatenate([final] * 4, axis=0).T
    most = jnp.maximum(jnp.max(stat[0], axis=0), jnp.max(stat[1], axis=0))[3:4]
    most = jnp.broadcast_to(jnp.maximum(most[:, 0:128], most[:, 128:256]), (8, 128))
    for turn_by in (32, 64):
        most = jnp.maximum(most, pltpu.roll(most, turn_by, axis=1))
    wide = jnp.concatenate([most, most], axis=1)[0:1]
    sums = jnp.zeros((1, 256), F32)
    for g in both:
        scaled = jnp.exp(stat[g, :, 3:4, :] - wide[None])
        part = (stat[g, :, 4:5, :] + stat[g, :, 5:6, :] + stat[g, :, 6:7, :]) * scaled
        sums += jnp.sum(part, axis=0)
    sums = jnp.broadcast_to(sums[:, 0:128] + sums[:, 128:256], (8, 128))
    for turn_by in (32, 64):
        sums += pltpu.roll(sums, turn_by, axis=1)
    final_lse = (most + jnp.log(sums))[0:1]

    def final_prob(i):
        rows = pl.ds(pl.multiple_of(i * TILE, TILE), TILE)
        fint[rows] = jnp.exp(fint[rows] - final_lse)

    each(0, SHARD // TILE, final_prob)

    each(4, 8, turn)
    landed(zx.at[0, pl.ds(1, 15)], zx_r.at[0])
    zz[0, 0] = jnp.sum(zx[0], axis=0)
    all_of(zz_copy, 0)

    lane128 = lax.broadcasted_iota(jnp.int32, (1, 128), 1)
    row8 = lax.broadcasted_iota(jnp.int32, (8, 256), 0)

    def log_total(g):
        value = jnp.log(jnp.sum(zz[g], axis=0))
        return jnp.concatenate([value[0:1], value[1:2]], axis=1)

    def slopes(g, lse):
        def body(i, carry):
            rows = pl.ds(pl.multiple_of(i * TILE, TILE), TILE)
            value = logits[g, rows]
            prob = jnp.exp(value - lse)
            target = jnp.concatenate([fint[rows], fint[rows]], axis=1)
            p0, p1 = prob[:, 0:128], prob[:, 128:256]
            if g == 1:
                follow = jnp.where(lane128 < 96, p1 - pltpu.roll(p0, 96, axis=1), 0.0)
                border[rows] = p0
            else:
                follow = p1 - pltpu.roll(jnp.where(lane128 < 32, border[rows], p0), 96, axis=1)
            slope = (prob - target) + jnp.concatenate([p0 - p1, follow], axis=1)
            grad[g, rows] = slope.astype(BF16)
            return carry + fold(slope * value)

        proj = jnp.sum(lax.fori_loop(0, SHARD // TILE, body, zero), axis=0, keepdims=True)
        high = proj.astype(BF16).astype(F32)
        return jnp.where(row8 == 0, high, proj - high)

    def product(g, tag, i):
        rows = pl.ds(pl.multiple_of(i * QUAD, 16), QUAD)
        value = jnp.dot(unt[rows, :], grad[g], preferred_element_type=F32)
        for w in range(4):
            one, two = value[STEP * w:STEP * w + HALF], value[STEP * w + HALF:STEP * w + WIN]
            if w < 2:
                two = jnp.concatenate([two[0:88], jnp.where(row8 < 2, tag, two[88:96])], axis=0)
            else:
                one = jnp.concatenate([jnp.where(row8 < 2, tag, one[0:8]), one[8:96]], axis=0)
            one, two = one.astype(BF16), two.astype(BF16)
            for p in both:
                gt[p, g, 0, i, w] = one[:, 128 * p:128 * p + 128]
                gt[p, g, 1, w, i] = two[:, 128 * p:128 * p + 128]

    def cross(g, h, d):
        i = (x + d) % 4
        src = gt.at[other, g, 0, i] if h == 0 else gt.at[other, g, 1, :, i]
        land = core_in.at[g, 0, i] if h == 0 else core_in.at[g, 1, :, i]
        return remote(src, land, ce_s.at[0], ce_r.at[g, d], sibling)

    def s_back(g, h, j, k):
        f, s = axes[h]
        to = (s + k) % 4
        if h == 0:
            n = (f + j) % 4
            return remote(gt.at[c, g, 0, n, to], sin.at[g, 0, k, n], ss_s.at[0], ss_r.at[g, 0],
                          place(h, f, to))
        return remote(gt.at[c, g, 1, :, to], sin.at[g, 1, k], ss_s.at[0], ss_r.at[g, 1],
                      place(h, f, to))

    def merge(g, d):
        i = (x + d) % 4
        landed(core_in.at[g, :, 0], ce_r.at[g, d])
        for w in range(4):
            gt[c, g, 0, i, w] = (gt[c, g, 0, i, w].astype(F32) + core_in[g, 0, i, w].astype(F32)).astype(BF16)
            gt[c, g, 1, w, i] = (gt[c, g, 1, w, i].astype(F32) + core_in[g, 1, w, i].astype(F32)).astype(BF16)
        for k in FAR:
            begin(s_back, g, 0, d, k)
        if d:
            begin(s_back, g, 1, 0, d)

    order = (2, 1, 3, 0)

    def backward(g, tag):
        for n, d in enumerate(order):
            product(g, tag, (x + d) % 4)
            for h in both:
                begin(cross, g, h, d)
            if n:
                merge(g, order[n - 1])
        merge(g, order[3])

    def f_back(g, h, k):
        f, s = axes[h]
        to = (f + k) % 4
        return remote(q.at[g, h, to], fzin.at[g, h, k], sf_s.at[0], sf_r.at[g, h], place(h, to, s))

    def scatter_s(g):
        for h in (1, 0):
            f, s = axes[h]
            landed(sin.at[g, h, pl.ds(1, 3)], ss_r.at[g, h])

            def total_of(n):
                value = gt[c, g, h, n, s].astype(F32)
                for k in (1, 2, 3):
                    value += sin[g, h, k, n].astype(F32)
                return value

            for k in FAR:
                n = (f + k) % 4
                q[g, h, n] = total_of(n).astype(BF16)
                begin(f_back, g, h, k)
            qown[g, h] = total_of(f)

    def fz_copy(g, k):
        to = 4 * g + k
        return remote(fz16.at[to], fzr.at[(to + 8 - z) % 8], fz_s.at[0], fz_r.at[0], (to * 2 + c, voc))

    def scatter_f(g):
        whole = []
        for h in both:
            landed(fzin.at[g, h, pl.ds(1, 3)], sf_r.at[g, h])
            whole.append(qown[g, h] + fzin[g, h, 1].astype(F32) + fzin[g, h, 2].astype(F32)
                         + fzin[g, h, 3].astype(F32))
        own_inv = jnp.where(c == 0, inv[g, :, 0:128], inv[g, :, 128:256])
        full = jnp.concatenate([*whole, own_inv, jnp.zeros((56, 128), F32)], axis=0).T
        fz32[4 * g:4 * g + 4] = full.reshape(4, ROWS, 256)
        fz16[4 * g:4 * g + 4] = full.reshape(4, ROWS, 256).astype(BF16)
        for k in range(4):
            @pl.when(z != 4 * g + k)
            def _():
                fz_copy(g, k).start()

    each(8, 11, turn)
    turn_last()
    landed(zz.at[1, pl.ds(1, 15)], zz_r.at[1])
    tag1 = slopes(1, log_total(1))
    backward(1, tag1)
    landed(zz.at[0, pl.ds(1, 15)], zz_r.at[0])
    tag0 = slopes(0, log_total(0))
    for n, d in enumerate(order):
        product(0, tag0, (x + d) % 4)
        for h in both:
            begin(cross, 0, h, d)
        if n:
            merge(0, order[n - 1])
    merge(0, order[3])
    scatter_s(1)
    scatter_s(0)
    scatter_f(1)
    scatter_f(0)

    grown = fz32[z]
    inv_col = grown[:, WIN:WIN + 1]
    landed(fzr.at[pl.ds(1, 7)], fz_r.at[0])
    for k in range(1, 8):
        grown += fzr[k].astype(F32)
    along = jnp.sum(jnp.where((lane == base) | (lane == base + 1), grown, 0.0), axis=1, keepdims=True)
    grown = pltpu.roll(grown, (256 - shift) % 256, axis=1)[:, 0:OWN]
    out_ref[...] = inv_col * gain[...] * grown - lens[:, 0:OWN] * (inv_col * inv_col * along / D)

    sent(zbuf.at[pl.ds(0, 7)], gz_s.at[0])
    sent(nt.at[c, :, :, 0, pl.ds(0, 3)], gf_s.at[0])
    sent(nt.at[c, :, :, pl.ds(0, 3)], gs_s.at[0])
    sent(nt.at[c], gc_s.at[0])
    sent(zx.at[:, pl.ds(1, 15)], zx_s.at[0])
    sent(zz.at[:, pl.ds(1, 15)], zz_s.at[0])
    sent(gt.at[other], ce_s.at[0])
    sent(gt.at[c, :, :, pl.ds(0, 3)], ss_s.at[0])
    sent(q.at[:, :, pl.ds(0, 3)], sf_s.at[0])
    sent(fz16.at[pl.ds(0, 7)], fz_s.at[0])


def weights(hid_ref, go_ref, out_ref, bias_ref):
    turned = go_ref[...].T
    bias_ref[...] = jnp.sum(go_ref[...], axis=0, keepdims=True)
    value = jnp.dot(turned.astype(BF16), hid_ref[...], preferred_element_type=F32)
    out_ref[...] = value.reshape(out_ref.shape)


def on_device(hidden, translator, bias, gain, unembed, final_logits):
    vmem, sem = pltpu.VMEM, pltpu.SemaphoreType.DMA
    anywhere = pl.BlockSpec(memory_space=pl.ANY)
    inside = pl.BlockSpec(memory_space=pltpu.VMEM)
    grad_out = pl.pallas_call(
        kernel,
        out_shape=pltpu.VMEM((ROWS, OWN), F32),
        in_specs=[anywhere] * 6,
        out_specs=inside,
        scratch_shapes=[
            vmem((ROWS, D), BF16), vmem((ROWS, 3072), F32), vmem((OWN, D), BF16),
            vmem((1, OWN), F32), vmem((1, OWN), F32),
            vmem((SHARD, D), BF16), vmem((D, SHARD), BF16),
            vmem((ROWS, SHARD), BF16), vmem((SHARD, 128), F32),
            vmem((ROWS, 256), F32), vmem((8, ROWS, 256), BF16),
            vmem((2, 2, 2, 4, 4, HALF, 128), BF16), vmem((2, D, 256), BF16),
            vmem((2, 16, 8, 256), F32), vmem((2, SHARD, 256), F32), vmem((2, 8, 256), F32),
            vmem((2, SHARD, 256), BF16), vmem((2, 2, 2, 4, 4, HALF, 128), BF16),
            vmem((2, 2, 4, 4, HALF, 128), BF16),
            vmem((SHARD, 128), F32), vmem((2, 16, 2, 128), F32), vmem((2, 16, 2, 128), F32),
            vmem((2, 2, 4, 4, HALF, 128), BF16),
            vmem((2, 2, 4, HALF, 128), BF16), vmem((2, 2, HALF, 128), F32),
            vmem((2, 2, 4, HALF, 128), BF16),
            vmem((8, ROWS, 256), F32), vmem((8, ROWS, 256), BF16), vmem((8, ROWS, 256), BF16),
            sem((6,)), sem((1,)), sem((2,)), sem((1,)), sem((2, 2, 3)),
            sem((1,)), sem((2, 2, 4)), sem((1,)), sem((2,)), sem((1,)), sem((2,)), sem((1,)), sem((2,)),
            sem((1,)), sem((2, 4)), sem((1,)), sem((2, 2)),
            sem((1,)), sem((2, 2)), sem((1,)), sem((1,)),
        ],
        compiler_params=pltpu.CompilerParams(
            collective_id=0, has_side_effects=True, vmem_limit_bytes=58 * 1024 * 1024),
    )(hidden[0], translator[0].T, bias, gain.reshape(1, OWN), unembed.T, final_logits)
    grad_translator, grad_bias = pl.pallas_call(
        weights,
        out_shape=(jax.ShapeDtypeStruct((OWN, 1, D), F32), jax.ShapeDtypeStruct((1, OWN), F32)),
        in_specs=[inside, inside],
        out_specs=(inside, inside),
        compiler_params=pltpu.CompilerParams(vmem_limit_bytes=32 * 1024 * 1024),
    )(hidden[0], grad_out)
    return jnp.transpose(grad_translator, (1, 2, 0)), grad_bias


def solution(mesh):
    placed = (
        P("layer", None, None),
        P("layer", None, "vocab"),
        P("layer", "vocab"),
        P("vocab"),
        P(None, ("layer", "vocab")),
        P(None, ("layer", "vocab")),
    )
    return jax.shard_map(
        on_device,
        mesh=mesh,
        in_specs=placed,
        out_specs=(P("layer", None, "vocab"), P("layer", "vocab")),
        check_vma=False,
    )
```

```python
import functools

import jax
import jax.numpy as jnp
from jax import lax
from jax.experimental import pallas as pl
from jax.experimental.pallas import tpu as pltpu
from jax.sharding import PartitionSpec as P

MESH = pl.DeviceIdType.MESH
F32, BF16 = jnp.float32, jnp.bfloat16
EPS = 1e-05
D, ROWS, OWN, SHARD = 2880, 32, 180, 784
WIN, HALF = 192, 96
STEP = 176
QUAD = 4 * OWN
TILE = 112
NEAR = (1, 3, 2)
FAR = (2, 1, 3)
PLANE = (10, 9, 11, 6, 14, 5, 7, 8, 2, 13, 15, 1, 3, 4, 12)
LINE = (8, 9, 7, 6, 10, 11, 5, 4, 12, 13, 3, 2, 14, 15, 1)


def split3(value):
    high = value.astype(BF16).astype(F32)
    rest = value - high
    mid = rest.astype(BF16).astype(F32)
    return high, mid, (rest - mid).astype(BF16).astype(F32)


def kernel(hid_h, trans_h, bias_h, gain_h, un_h, fin_h, out_ref,
           hid, hpad, trans, bias, gain, un, unt, fin, fint,
           lens, zbuf, nt, dense, stat, logits, inv, grad, gt, core_in,
           border, zx, zz, sin, q, qown, fzin, fz32, fz16, fzr,
           local, gz_s, gz_r, gf_s, gf_r, gs_s, gs_r, gc_s, gc_r, zx_s, zx_r, zz_s, zz_r,
           ce_s, ce_r, ss_s, ss_r, sf_s, sf_r, fz_s, fz_r):
    layer, voc = lax.axis_index("layer"), lax.axis_index("vocab")
    z, c = layer // 2, layer % 2
    x, y = voc // 4, voc % 4
    other = 1 - c
    sibling = (z * 2 + other, voc)

    def remote(src, dst, send, recv, device):
        return pltpu.make_async_remote_copy(
            src_ref=src, dst_ref=dst, send_sem=send, recv_sem=recv,
            device_id=device, device_id_type=MESH)

    def begin(copy, *at):
        copy(*at).start()

    def sent(ref, semaphore):
        remote(ref, ref, semaphore, semaphore, sibling).wait_send()

    def landed(ref, semaphore):
        remote(ref, ref, semaphore, semaphore, sibling).wait_recv()

    def each(lo, hi, act):
        def body(k, _):
            act(k)
            return 0
        lax.fori_loop(lo, hi, body, 0)

    barrier = pltpu.get_barrier_semaphore()

    def greet(k):
        pl.semaphore_signal(barrier, inc=1, device_id=((layer + k) % 16, voc), device_id_type=MESH)
        pl.semaphore_signal(barrier, inc=1, device_id=(layer, (voc + k) % 16), device_id_type=MESH)

    loads = [pltpu.make_async_copy(a, b, local.at[i]) for i, (a, b) in enumerate(
        [(trans_h, trans), (hid_h, hid), (bias_h, bias), (gain_h, gain), (fin_h, fin)])]
    parts = [pltpu.make_async_copy(un_h.at[pl.ds(i * TILE, TILE)], un.at[pl.ds(i * TILE, TILE)], local.at[5])
             for i in range(SHARD // TILE)]
    for load in loads:
        load.start()
    each(1, 16, greet)

    loads[4].wait()
    final = fin[...].astype(F32)
    top = jnp.max(final, axis=1, keepdims=True)
    total = jnp.sum(jnp.exp(final - top), axis=1, keepdims=True)

    for load in loads[:4]:
        load.wait()
    hpad[:, 2688:3072] = jnp.zeros((ROWS, 384), F32)
    hpad[:, 0:D] = hid[...].astype(F32)
    first = voc * OWN
    tile = first // 128
    near = hpad[:, pl.ds(pl.multiple_of(tile * 128, 128), 384)]
    own = pltpu.roll(near, (384 - (first - tile * 128)) % 384, axis=1)[:, 0:OWN]
    lens_out = own + lax.dot_general(hid[...], trans[...], (((1,), (1,)), ((), ())),
                                     preferred_element_type=F32) + bias[...]
    shift = y * 4
    base = jnp.where(y < 2, 184, 0)
    lens[...] = jnp.zeros_like(lens)
    lens[:, 0:OWN] = lens_out * gain[...]
    pay = pltpu.roll(lens[...], shift, axis=1)
    lens[:, 0:OWN] = lens_out
    squares = jnp.sum(lens_out * lens_out, axis=1, keepdims=True)
    lane = lax.broadcasted_iota(jnp.int32, (ROWS, 256), 1)
    for k, value in enumerate((*split3(squares), top, *split3(total))):
        pay = jnp.where(lane == base + k, value, pay)
    zbuf[z] = pay.astype(BF16)

    pl.semaphore_wait(barrier, 30)

    def z_send(k):
        return remote(zbuf.at[z], zbuf.at[z], gz_s.at[0], gz_r.at[z // 4], (((z + k) % 8) * 2 + c, voc))

    def z_come(g):
        @pl.when(z // 4 == g)
        def _():
            landed(zbuf.at[pl.ds(4 * g, 3)], gz_r.at[g])

        @pl.when(z // 4 != g)
        def _():
            landed(zbuf.at[pl.ds(4 * g, 4)], gz_r.at[g])

    for k in (4, 3, 5, 2, 6, 1, 7):
        begin(z_send, k)
    for part in parts:
        part.start()

    axes = ((x, y), (y, x))

    def place(h, f, s):
        return (layer, f * 4 + s) if h == 0 else (layer, s * 4 + f)

    def f_send(g, h, k):
        f, s = axes[h]
        src = nt.at[c, g, h, f, s]
        return remote(src, src, gf_s.at[0], gf_r.at[g, h, k - 1], place(h, (f + k) % 4, s))

    def f_come(g, h, k):
        f, s = axes[h]
        land = nt.at[c, g, h, (f + 4 - k) % 4, s]
        landed(land, gf_r.at[g, h, k - 1])

    def s_send(g, h, j, k):
        f, s = axes[h]
        src = nt.at[c, g, h, (f + 4 - j) % 4, s]
        return remote(src, src, gs_s.at[0], gs_r.at[g, h, j], place(h, f, (s + k) % 4))

    def s_come(g, h, j):
        f, s = axes[h]
        landed(nt.at[c, g, h, (f + 4 - j) % 4, pl.ds(0, 3)], gs_r.at[g, h, j])

    def share(g, h, j):
        f, s = axes[h]
        src = nt.at[c, g, h, (f + 4 - j) % 4]
        return remote(src, src, gc_s.at[0], gc_r.at[g], sibling)

    def share_come(g):
        landed(nt.at[other, g], gc_r.at[g])

    both = (0, 1)

    def gather_own(g):
        z_come(g)
        turned = zbuf[4 * g:4 * g + 4].astype(F32).reshape(128, 256).T.astype(BF16)
        nt[c, g, 0, x, y] = turned[0:HALF]
        nt[c, g, 1, y, x] = turned[HALF:WIN]
        for k in FAR:
            for h in both:
                begin(f_send, g, h, k)
        for k in FAR:
            for h in both:
                begin(s_send, g, h, 0, k)

    def gather_on(g):
        for j in NEAR:
            for h in both:
                f_come(g, h, j)
                for k in FAR:
                    begin(s_send, g, h, j, k)

    def gather_end_part(g, n):
        for h in both:
            s_come(g, h, (0, *NEAR)[n])
            begin(share, g, h, (0, *NEAR)[n])

    def gather_end(g):
        for n in range(4):
            gather_end_part(g, n)

    row16 = lax.broadcasted_iota(jnp.int32, (16, 128), 0)

    def join(g, p):
        cols = pl.ds(pl.multiple_of(128 * p, 128), 128)

        def body(i):
            if True:
                for w in range(4):
                    at = pl.multiple_of(i * QUAD, 16) + STEP * w
                    head = nt[p, g, 0, i, w, 0:16]
                    if w:
                        tail = nt[p, g, 1, w - 1, i, 80:96]
                        head = jnp.where(row16 < 4 * w, tail.astype(F32), head.astype(F32)).astype(BF16)
                    dense[g, pl.ds(at, 16), cols] = head
                    dense[g, pl.ds(at + 16, 80), cols] = nt[p, g, 0, i, w, 16:96]
                    if w < 3:
                        dense[g, pl.ds(at + 96, 80), cols] = nt[p, g, 1, w, i, 0:80]
                    else:
                        dense[g, pl.ds(at + 96, 96), cols] = nt[p, g, 1, w, i]
                    if w < 2:
                        piece = nt[p, g, 1, w, i, 80:96].astype(F32)[8:16]
                    else:
                        piece = nt[p, g, 0, i, w, 0:16].astype(F32)[0:8]
                    stat[g, i * 4 + w, :, cols] = piece

        each(0, 4, body)

    def norms(g):
        sums = jnp.sum(stat[g], axis=0)
        inv[g] = jnp.broadcast_to(lax.rsqrt((sums[0:1] + sums[1:2] + sums[2:3]) / D + EPS), (8, 256))

    def fold(value):
        return jnp.sum(value.reshape(TILE // 8, 8, 256), axis=0)

    zero = jnp.zeros((8, 256), F32)

    def product_of(g, n):
        at, depth = ((0, 768), (768, 768), (1536, 768), (2304, 576))[n]
        part = jnp.dot(un[:, at:at + depth], dense[g, at:at + depth], preferred_element_type=F32)
        if n:
            logits[g] += part
        else:
            logits[g] = part

    def exps(g):
        def body(i, carry):
            rows = pl.ds(pl.multiple_of(i * TILE, TILE), TILE)
            value = logits[g, rows] * inv[g, 0:1]
            logits[g, rows] = value
            return carry + fold(jnp.exp(value))

        sums = jnp.sum(lax.fori_loop(0, SHARD // TILE, body, zero), axis=0, keepdims=True)
        zx[g, 0] = jnp.concatenate([sums[:, 0:128], sums[:, 128:256]], axis=0)

    def zx_copy(g, k):
        return remote(zx.at[g, 0], zx.at[g, k], zx_s.at[0], zx_r.at[g], (layer, (voc + k) % 16))

    def zz_copy(g, k):
        return remote(zz.at[g, 0], zz.at[g, k], zz_s.at[0], zz_r.at[g], ((layer + k) % 16, voc))

    def all_of(copy, g):
        for k in PLANE if copy is zx_copy else LINE:
            copy(g, k).start()


    eye = (lax.broadcasted_iota(jnp.int32, (256, 256), 0)
           == lax.broadcasted_iota(jnp.int32, (256, 256), 1)).astype(BF16)

    def turn(i):
        at = pl.multiple_of(i * 256, 256)
        unt[pl.ds(at, 256), :] = lax.dot_general(
            eye, un[:, pl.ds(at, 256)], (((1,), (1,)), ((), ())),
            preferred_element_type=F32).astype(BF16)

    def turn_last():
        unt[2816:D, :] = lax.dot_general(
            eye[0:64, 0:64], un[:, 2816:D], (((1,), (1,)), ((), ())),
            preferred_element_type=F32).astype(BF16)

    gather_own(1)
    gather_own(0)
    gather_on(1)
    gather_on(0)
    pltpu.make_async_copy(un_h, un, local.at[5]).wait()
    each(0, 4, turn)
    gather_end(1)
    join(1, c)
    share_come(1)
    join(1, other)
    norms(1)
    for n in range(4):
        product_of(1, n)
        gather_end_part(0, n)
    exps(1)
    all_of(zx_copy, 1)
    join(0, c)
    share_come(0)
    join(0, other)
    norms(0)
    for n in range(4):
        product_of(0, n)
    exps(0)
    all_of(zx_copy, 0)
    each(4, 6, turn)
    landed(zx.at[1, pl.ds(1, 15)], zx_r.at[1])
    zz[1, 0] = jnp.sum(zx[1], axis=0)
    all_of(zz_copy, 1)

    fint[...] = jnp.concatenate([final] * 4, axis=0).T
    most = jnp.maximum(jnp.max(stat[0], axis=0), jnp.max(stat[1], axis=0))[3:4]
    most = jnp.broadcast_to(jnp.maximum(most[:, 0:128], most[:, 128:256]), (8, 128))
    for turn_by in (32, 64):
        most = jnp.maximum(most, pltpu.roll(most, turn_by, axis=1))
    wide = jnp.concatenate([most, most], axis=1)[0:1]
    sums = jnp.zeros((1, 256), F32)
    for g in both:
        scaled = jnp.exp(stat[g, :, 3:4, :] - wide[None])
        part = (stat[g, :, 4:5, :] + stat[g, :, 5:6, :] + stat[g, :, 6:7, :]) * scaled
        sums += jnp.sum(part, axis=0)
    sums = jnp.broadcast_to(sums[:, 0:128] + sums[:, 128:256], (8, 128))
    for turn_by in (32, 64):
        sums += pltpu.roll(sums, turn_by, axis=1)
    final_lse = (most + jnp.log(sums))[0:1]

    def final_prob(i):
        rows = pl.ds(pl.multiple_of(i * TILE, TILE), TILE)
        fint[rows] = jnp.exp(fint[rows] - final_lse)

    each(0, SHARD // TILE, final_prob)

    each(6, 11, turn)
    turn_last()
    landed(zx.at[0, pl.ds(1, 15)], zx_r.at[0])
    zz[0, 0] = jnp.sum(zx[0], axis=0)
    all_of(zz_copy, 0)

    lane128 = lax.broadcasted_iota(jnp.int32, (1, 128), 1)
    row8 = lax.broadcasted_iota(jnp.int32, (8, 256), 0)

    def log_total(g):
        value = jnp.log(jnp.sum(zz[g], axis=0))
        return jnp.concatenate([value[0:1], value[1:2]], axis=1)

    def slopes(g, lse):
        def body(i, carry):
            rows = pl.ds(pl.multiple_of(i * TILE, TILE), TILE)
            value = logits[g, rows]
            prob = jnp.exp(value - lse)
            target = jnp.concatenate([fint[rows], fint[rows]], axis=1)
            p0, p1 = prob[:, 0:128], prob[:, 128:256]
            if g == 1:
                follow = jnp.where(lane128 < 96, p1 - pltpu.roll(p0, 96, axis=1), 0.0)
                border[rows] = p0
            else:
                follow = p1 - pltpu.roll(jnp.where(lane128 < 32, border[rows], p0), 96, axis=1)
            slope = (prob - target) + jnp.concatenate([p0 - p1, follow], axis=1)
            grad[g, rows] = slope.astype(BF16)
            return carry + fold(slope * value)

        proj = jnp.sum(lax.fori_loop(0, SHARD // TILE, body, zero), axis=0, keepdims=True)
        high = proj.astype(BF16).astype(F32)
        return jnp.where(row8 == 0, high, proj - high)

    def product(g, tag, i):
        rows = pl.ds(pl.multiple_of(i * QUAD, 16), QUAD)
        value = jnp.dot(unt[rows, :], grad[g], preferred_element_type=F32)
        for w in range(4):
            one, two = value[STEP * w:STEP * w + HALF], value[STEP * w + HALF:STEP * w + WIN]
            if w < 2:
                two = jnp.concatenate([two[0:88], jnp.where(row8 < 2, tag, two[88:96])], axis=0)
            else:
                one = jnp.concatenate([jnp.where(row8 < 2, tag, one[0:8]), one[8:96]], axis=0)
            one, two = one.astype(BF16), two.astype(BF16)
            for p in both:
                gt[p, g, 0, i, w] = one[:, 128 * p:128 * p + 128]
                gt[p, g, 1, w, i] = two[:, 128 * p:128 * p + 128]

    def cross(g, h, d):
        i = (x + d) % 4
        src = gt.at[other, g, 0, i] if h == 0 else gt.at[other, g, 1, :, i]
        land = core_in.at[g, 0, i] if h == 0 else core_in.at[g, 1, :, i]
        return remote(src, land, ce_s.at[0], ce_r.at[g, d], sibling)

    def s_back(g, h, j, k):
        f, s = axes[h]
        to = (s + k) % 4
        if h == 0:
            n = (f + j) % 4
            return remote(gt.at[c, g, 0, n, to], sin.at[g, 0, k, n], ss_s.at[0], ss_r.at[g, 0],
                          place(h, f, to))
        return remote(gt.at[c, g, 1, :, to], sin.at[g, 1, k], ss_s.at[0], ss_r.at[g, 1],
                      place(h, f, to))

    def merge(g, d):
        i = (x + d) % 4
        landed(core_in.at[g, :, 0], ce_r.at[g, d])
        for w in range(4):
            gt[c, g, 0, i, w] = (gt[c, g, 0, i, w].astype(F32) + core_in[g, 0, i, w].astype(F32)).astype(BF16)
            gt[c, g, 1, w, i] = (gt[c, g, 1, w, i].astype(F32) + core_in[g, 1, w, i].astype(F32)).astype(BF16)
        for k in FAR:
            begin(s_back, g, 0, d, k)
        if d:
            begin(s_back, g, 1, 0, d)

    order = (2, 1, 3, 0)

    def backward(g, tag):
        for n, d in enumerate(order):
            product(g, tag, (x + d) % 4)
            for h in both:
                begin(cross, g, h, d)
            if n > 1:
                merge(g, order[n - 2])

    def f_back(g, h, k):
        f, s = axes[h]
        to = (f + k) % 4
        return remote(q.at[g, h, to], fzin.at[g, h, k], sf_s.at[0], sf_r.at[g, h], place(h, to, s))

    def scatter_s(g):
        for h in (1, 0):
            f, s = axes[h]
            landed(sin.at[g, h, pl.ds(1, 3)], ss_r.at[g, h])

            def total_of(n):
                value = gt[c, g, h, n, s].astype(F32)
                for k in (1, 2, 3):
                    value += sin[g, h, k, n].astype(F32)
                return value

            for k in FAR:
                n = (f + k) % 4
                q[g, h, n] = total_of(n).astype(BF16)
                begin(f_back, g, h, k)
            qown[g, h] = total_of(f)

    def fz_copy(g, k):
        to = 4 * g + k
        return remote(fz16.at[to], fzr.at[(to + 8 - z) % 8], fz_s.at[0], fz_r.at[0], (to * 2 + c, voc))

    def scatter_f(g):
        whole = []
        for h in both:
            landed(fzin.at[g, h, pl.ds(1, 3)], sf_r.at[g, h])
            whole.append(qown[g, h] + fzin[g, h, 1].astype(F32) + fzin[g, h, 2].astype(F32)
                         + fzin[g, h, 3].astype(F32))
        own_inv = jnp.where(c == 0, inv[g, :, 0:128], inv[g, :, 128:256])
        full = jnp.concatenate([*whole, own_inv, jnp.zeros((56, 128), F32)], axis=0).T
        fz32[4 * g:4 * g + 4] = full.reshape(4, ROWS, 256)
        fz16[4 * g:4 * g + 4] = full.reshape(4, ROWS, 256).astype(BF16)
        for k in range(4):
            @pl.when(z != 4 * g + k)
            def _():
                fz_copy(g, k).start()

    landed(zz.at[1, pl.ds(1, 15)], zz_r.at[1])
    tag1 = slopes(1, log_total(1))
    backward(1, tag1)
    landed(zz.at[0, pl.ds(1, 15)], zz_r.at[0])
    merge(1, order[2])
    tag0 = slopes(0, log_total(0))
    merge(1, order[3])
    for n, d in enumerate(order):
        product(0, tag0, (x + d) % 4)
        for h in both:
            begin(cross, 0, h, d)
        if n:
            merge(0, order[n - 1])
    merge(0, order[3])
    scatter_s(1)
    scatter_s(0)
    scatter_f(1)
    scatter_f(0)

    grown = fz32[z]
    inv_col = grown[:, WIN:WIN + 1]
    landed(fzr.at[pl.ds(1, 7)], fz_r.at[0])
    for k in range(1, 8):
        grown += fzr[k].astype(F32)
    along = jnp.sum(jnp.where((lane == base) | (lane == base + 1), grown, 0.0), axis=1, keepdims=True)
    grown = pltpu.roll(grown, (256 - shift) % 256, axis=1)[:, 0:OWN]
    out_ref[...] = inv_col * gain[...] * grown - lens[:, 0:OWN] * (inv_col * inv_col * along / D)

    sent(zbuf.at[pl.ds(0, 7)], gz_s.at[0])
    sent(nt.at[c, :, :, 0, pl.ds(0, 3)], gf_s.at[0])
    sent(nt.at[c, :, :, pl.ds(0, 3)], gs_s.at[0])
    sent(nt.at[c], gc_s.at[0])
    sent(zx.at[:, pl.ds(1, 15)], zx_s.at[0])
    sent(zz.at[:, pl.ds(1, 15)], zz_s.at[0])
    sent(gt.at[other], ce_s.at[0])
    sent(gt.at[c, :, :, pl.ds(0, 3)], ss_s.at[0])
    sent(q.at[:, :, pl.ds(0, 3)], sf_s.at[0])
    sent(fz16.at[pl.ds(0, 7)], fz_s.at[0])


def weights(hid_ref, go_ref, out_ref, bias_ref):
    turned = go_ref[...].T
    bias_ref[...] = jnp.sum(go_ref[...], axis=0, keepdims=True)
    value = jnp.dot(turned.astype(BF16), hid_ref[...], preferred_element_type=F32)
    out_ref[...] = value.reshape(out_ref.shape)


def on_device(hidden, translator, bias, gain, unembed, final_logits):
    vmem, sem = pltpu.VMEM, pltpu.SemaphoreType.DMA
    anywhere = pl.BlockSpec(memory_space=pl.ANY)
    inside = pl.BlockSpec(memory_space=pltpu.VMEM)
    grad_out = pl.pallas_call(
        kernel,
        out_shape=pltpu.VMEM((ROWS, OWN), F32),
        in_specs=[anywhere] * 6,
        out_specs=inside,
        scratch_shapes=[
            vmem((ROWS, D), BF16), vmem((ROWS, 3072), F32), vmem((OWN, D), BF16),
            vmem((1, OWN), F32), vmem((1, OWN), F32),
            vmem((SHARD, D), BF16), vmem((D, SHARD), BF16),
            vmem((ROWS, SHARD), BF16), vmem((SHARD, 128), F32),
            vmem((ROWS, 256), F32), vmem((8, ROWS, 256), BF16),
            vmem((2, 2, 2, 4, 4, HALF, 128), BF16), vmem((2, D, 256), BF16),
            vmem((2, 16, 8, 256), F32), vmem((2, SHARD, 256), F32), vmem((2, 8, 256), F32),
            vmem((2, SHARD, 256), BF16), vmem((2, 2, 2, 4, 4, HALF, 128), BF16),
            vmem((2, 2, 4, 4, HALF, 128), BF16),
            vmem((SHARD, 128), F32), vmem((2, 16, 2, 128), F32), vmem((2, 16, 2, 128), F32),
            vmem((2, 2, 4, 4, HALF, 128), BF16),
            vmem((2, 2, 4, HALF, 128), BF16), vmem((2, 2, HALF, 128), F32),
            vmem((2, 2, 4, HALF, 128), BF16),
            vmem((8, ROWS, 256), F32), vmem((8, ROWS, 256), BF16), vmem((8, ROWS, 256), BF16),
            sem((6,)), sem((1,)), sem((2,)), sem((1,)), sem((2, 2, 3)),
            sem((1,)), sem((2, 2, 4)), sem((1,)), sem((2,)), sem((1,)), sem((2,)), sem((1,)), sem((2,)),
            sem((1,)), sem((2, 4)), sem((1,)), sem((2, 2)),
            sem((1,)), sem((2, 2)), sem((1,)), sem((1,)),
        ],
        compiler_params=pltpu.CompilerParams(
            collective_id=0, has_side_effects=True, vmem_limit_bytes=58 * 1024 * 1024),
    )(hidden[0], translator[0].T, bias, gain.reshape(1, OWN), unembed.T, final_logits)
    grad_translator, grad_bias = pl.pallas_call(
        weights,
        out_shape=(jax.ShapeDtypeStruct((OWN, 1, D), F32), jax.ShapeDtypeStruct((1, OWN), F32)),
        in_specs=[inside, inside],
        out_specs=(inside, inside),
        compiler_params=pltpu.CompilerParams(vmem_limit_bytes=32 * 1024 * 1024),
    )(hidden[0], grad_out)
    return jnp.transpose(grad_translator, (1, 2, 0)), grad_bias


def solution(mesh):
    placed = (
        P("layer", None, None),
        P("layer", None, "vocab"),
        P("layer", "vocab"),
        P("vocab"),
        P(None, ("layer", "vocab")),
        P(None, ("layer", "vocab")),
    )
    return jax.shard_map(
        on_device,
        mesh=mesh,
        in_specs=placed,
        out_specs=(P("layer", None, "vocab"), P("layer", "vocab")),
        check_vma=False,
    )
```
